32 devices in a mesh: groups: 2 (over y), dp: 4 (over x, core), tensor: 4 (over z).
Axes of the slice: x: 2, y: 2, z: 4, core: 2. Of those that a mesh axis runs over, the one named last changes fastest.
Arguments:
- inputs: bfloat16 [4096, 3072], P(('groups', 'dp', 'tensor')), parts along dimension 0, may hold values from -40 to 40
- grad_out: bfloat16 [4096, 3072], P(('groups', 'dp', 'tensor')), parts along dimension 0, may hold values from -6 to 6
- norm_gain: float32 [3072], replicated, may hold values from 0.5 to 1.5
- level_order: int32 [4096], P(('groups', 'dp')), parts along dimension 0, may hold values from 0 to 511, as said below
- level_counts: int32 [8, 4], P(('groups', 'dp')), parts along dimension 0, may hold values from 0 to 256, as said below
- weight_in: bfloat16 [3072, 12288], P(None, 'tensor'), may hold values from -0.109375 to 0.109375
- weight_out: bfloat16 [12288, 3072], P('tensor'), may hold values from -0.0546875 to 0.0546875
Outputs:
- grad_input: bfloat16 [4096, 3072], P(('groups', 'dp', 'tensor')), parts along dimension 0
- grad_weight_in: bfloat16 [6144, 12288], P(('groups', 'dp'), 'tensor'), parts along dimension 0
- grad_weight_out: bfloat16 [24576, 3072], P(('groups', 'tensor'), 'dp'), parts along dimension 0
The draws below stay inside these ranges and needn't reach their ends.
There are 2 independent parts, one for each index of `groups`. The reference program is written for one: setup_inputs(seed, part) draws one part's arguments, and reference() takes and returns one part's arrays. A program takes and returns all parts, laid end to end along the dimension named above; an argument that names none is the same for every part. Nothing has to cross between parts.
Inputs may be any that keep to these rules, and one draw needn't show every extreme that they name: `level_order`: within each aligned block of 512 entries a permutation of 0 to 511; within one level the indices rise. `level_counts`: row b holds the numbers of tokens of levels 0, 1, 2, 3 in block b and sums to 512; counts[b, 3] <= 128, counts[b, 3] + counts[b, 2] <= 256, counts[b, 3] + counts[b, 2] + counts[b, 1] <= 384, each bound met with equality in some block.
All inputs are finite; a program needn't handle non-finite values.
Results may differ from the reference program's by a relative error of at most 0.009.
Values may be sent and summed in bfloat16 or wider, within the bound.
No kernel may reach another device: no remote copies, remote signals or barrier semaphores. Data moves between devices by JAX's collectives and lax.ppermute only.
A program may use at most 256 MiB of HBM per device.

```python
import math
import jax
import jax.numpy as jnp
from jax import lax

D = 3072
FF = 12288
TOK_DEV = 512
BLOCKS = 4
TOKENS = 2048


def level_plan(key):
    quarter = TOK_DEV // 4
    eighth = TOK_DEV // 8
    key_top, key_mid, key_low, key_pick, key_perm = jax.random.split(key, 5)
    above_three = jax.random.randint(key_top, (BLOCKS,), eighth, quarter + 1)
    above_two = jax.random.randint(key_mid, (BLOCKS,), quarter, 2 * quarter + 1)
    above_one = jax.random.randint(key_low, (BLOCKS,), 2 * quarter, 3 * quarter + 1)
    picks = jax.random.permutation(key_pick, BLOCKS)
    block_ids = jnp.arange(BLOCKS)
    full_block = block_ids == picks[0]
    light_block = block_ids == picks[1]
    above_three = jnp.where(full_block, quarter, jnp.where(light_block, eighth, above_three))
    above_two = jnp.where(full_block | light_block, 2 * quarter, above_two)
    above_one = jnp.where(full_block, 3 * quarter, jnp.where(light_block, 2 * quarter, above_one))
    block_keys = jax.random.split(key_perm, BLOCKS)
    shuffles = jax.vmap(lambda one_key: jax.random.permutation(one_key, TOK_DEV))(block_keys)
    places = jnp.argsort(shuffles, axis=1)
    token_level = (places < above_three[:, None]).astype(jnp.int32) + (places < above_two[:, None]).astype(jnp.int32) + (places < above_one[:, None]).astype(jnp.int32)
    sort_keys = (3 - token_level) * TOK_DEV + jnp.arange(TOK_DEV, dtype=jnp.int32)[None, :]
    ordering = jnp.argsort(sort_keys, axis=1).astype(jnp.int32)
    tallies = jnp.stack([TOK_DEV - above_one, above_one - above_two, above_two - above_three, above_three], axis=1).astype(jnp.int32)
    return (ordering.reshape(TOKENS), tallies)


def draw_level_order(key, part):
    plan = level_plan(key)
    return plan[0]


def draw_level_counts(key, part):
    plan = level_plan(key)
    return plan[1]


def draw_inputs(key, part):
    key = jax.random.fold_in(key, 17)
    key_base, key_rough, key_rows = jax.random.split(key, 3)
    position = jnp.arange(D, dtype=jnp.float32) / D
    rough = jax.random.uniform(key_rough, (1, D), jnp.float32, 0.7, 1.4)
    base = jnp.clip(jax.random.normal(key_base, (TOKENS, D), jnp.float32), -5.0, 5.0)
    rising = jnp.exp(position * math.log(10.0))[None, :]
    row_scale = jnp.exp(jax.random.uniform(key_rows, (TOKENS, 1), jnp.float32, math.log(0.05), math.log(0.5)))
    return (row_scale * (base * rough * rising)).astype(jnp.bfloat16)


def levels(stream_key, extent, cuts, least, largest):
    level, own = 1.0, jax.random.fold_in(stream_key, 6)
    for axis_at, blocks in cuts:
        steps = jnp.exp(jax.random.uniform(jax.random.fold_in(own, axis_at), (blocks,), jnp.float32, least / len(cuts), largest / len(cuts)))
        level = level * jnp.repeat(steps, extent[axis_at] // blocks).reshape([-1 if axis == axis_at else 1 for axis in range(len(extent))])
    return level


def normal_values(own_key, extent, scale, most, cuts=(), kind=jnp.bfloat16):
    result = jax.random.normal(own_key, extent, jnp.float32) * scale
    if len(cuts) > 0:
        result = levels(own_key, extent, cuts, -0.22, 0.18) * result
    return jnp.clip(result, min=-most, max=most).astype(kind)


def setup_inputs(seed: int = 0, part: int = 0) -> dict:
    key_list = jax.random.split(jax.random.key(seed), 8)
    part_splits = jax.random.split(jax.random.fold_in(key_list[7], part), 8)
    inputs = draw_inputs(jax.random.fold_in(jax.random.fold_in(key_list[7], part), 71), part)
    grad_out = normal_values(part_splits[1], (TOKENS, D), 1.0, 6.0, ((0, 16),))
    norm_gain = jnp.clip(1.0 + 0.1 * jax.random.normal(key_list[2], (D,), jnp.float32), 0.5, 1.5)
    level_order = draw_level_order(jax.random.fold_in(jax.random.fold_in(key_list[7], part), 71), part)
    level_counts = draw_level_counts(jax.random.fold_in(jax.random.fold_in(key_list[7], part), 71), part)
    weight_in = normal_values(key_list[5], (D, FF), D ** -0.5, 0.109375, ((1, 4),))
    weight_out = normal_values(key_list[6], (FF, D), FF ** -0.5, 0.0546875, ((0, 4),))
    return {"inputs": inputs, "grad_out": grad_out, "norm_gain": norm_gain, "level_order": level_order, "level_counts": level_counts, "weight_in": weight_in, "weight_out": weight_out}


GELU_SCALE = 0.7978845608028654
GELU_CUBE = 0.044715
NORM_EPS = 1e-06

def gelu_parts(pre_act):
    tanh_val = jnp.tanh(GELU_SCALE * (pre_act + GELU_CUBE * pre_act * pre_act * pre_act))
    gelu_value = 0.5 * pre_act * (1.0 + tanh_val)
    gelu_slope = 0.5 * (1.0 + tanh_val) + 0.5 * pre_act * (1.0 - tanh_val * tanh_val) * GELU_SCALE * (1.0 + 3.0 * GELU_CUBE * pre_act * pre_act)
    return (gelu_value, gelu_slope)

def token_levels(block_order, count_row):
    above_three = count_row[3]
    above_two = above_three + count_row[2]
    above_one = above_two + count_row[1]
    places = jnp.arange(block_order.shape[0], dtype=jnp.int32)
    ranked = (places < above_three).astype(jnp.int32) + (places < above_two).astype(jnp.int32) + (places < above_one).astype(jnp.int32)
    return jnp.zeros(block_order.shape[0], jnp.int32).at[block_order].set(ranked)

def column_bands(first_column, column_count, unit_total):
    columns = first_column + jnp.arange(column_count, dtype=jnp.int32)
    return (columns >= unit_total // 8).astype(jnp.int32) + (columns >= unit_total // 4).astype(jnp.int32) + (columns >= unit_total // 2).astype(jnp.int32)

def norm_backward(grad_normed, standard, row_scale, norm_gain):
    scaled = grad_normed * norm_gain[None, :]
    centre = lax.optimization_barrier(jnp.mean(scaled, axis=1, keepdims=True))
    along = lax.optimization_barrier(jnp.mean(scaled * standard, axis=1, keepdims=True))
    return row_scale * (scaled - centre - standard * along)

def reference(inputs, grad_out, norm_gain, level_order, level_counts, weight_in, weight_out):
    unit_total = weight_in.shape[1]
    feature_count = inputs.shape[1]
    unit_band = column_bands(0, unit_total, unit_total)

    def one_block(totals, pieces):
        block_inputs, block_grads, block_order, count_row = pieces
        token_level = token_levels(block_order, count_row)
        unit_mask = unit_band[None, :] <= token_level[:, None]
        as_float = block_inputs.astype(jnp.float32)
        row_mean = lax.optimization_barrier(jnp.mean(as_float, axis=1, keepdims=True))
        centred = as_float - row_mean
        row_scale = lax.rsqrt(lax.optimization_barrier(jnp.mean(centred * centred, axis=1, keepdims=True)) + NORM_EPS)
        standard = centred * row_scale
        normed = (standard * norm_gain[None, :]).astype(jnp.bfloat16)
        pre_act = jnp.dot(normed, weight_in, preferred_element_type=jnp.float32)
        gelu_value, gelu_slope = gelu_parts(pre_act)
        hidden = jnp.where(unit_mask, gelu_value, 0.0).astype(jnp.bfloat16)
        grad_hidden = jnp.dot(block_grads, weight_out.T, preferred_element_type=jnp.float32)
        grad_pre = jnp.where(unit_mask, grad_hidden * gelu_slope, 0.0).astype(jnp.bfloat16)
        grad_normed = jnp.dot(grad_pre, weight_in.T, preferred_element_type=jnp.float32)
        grad_block = (block_grads.astype(jnp.float32) + norm_backward(grad_normed, standard, row_scale, norm_gain)).astype(jnp.bfloat16)
        in_part = jnp.dot(normed.T, grad_pre, preferred_element_type=jnp.float32)
        out_part = jnp.dot(hidden.T, block_grads, preferred_element_type=jnp.float32)
        in_part = lax.optimization_barrier(in_part.astype(jnp.bfloat16)).astype(jnp.float32)
        out_part = lax.optimization_barrier(out_part.astype(jnp.bfloat16)).astype(jnp.float32)
        return ((totals[0] + in_part, totals[1] + out_part), grad_block)
    start_totals = (jnp.zeros((feature_count, unit_total), jnp.float32), jnp.zeros((unit_total, feature_count), jnp.float32))
    pieces = (inputs.reshape(BLOCKS, TOK_DEV, feature_count), grad_out.reshape(BLOCKS, TOK_DEV, feature_count), level_order.reshape(BLOCKS, TOK_DEV), level_counts)
    totals, grad_blocks = lax.scan(one_block, start_totals, pieces)
    grad_input = grad_blocks.reshape(TOKENS, feature_count)
    grad_weight_in = (totals[0] / BLOCKS).astype(jnp.bfloat16)
    grad_weight_out = (totals[1] / BLOCKS).astype(jnp.bfloat16)
    return (grad_input, grad_weight_in, grad_weight_out)
```

```python
import jax
import jax.numpy as jnp
from jax import lax
from jax.sharding import PartitionSpec as P

GELU_SCALE = 0.7978845608028654
GELU_CUBE = 0.044715
NORM_EPS = 1e-06


def gelu_parts(pre_act):
    tanh_val = jnp.tanh(GELU_SCALE * (pre_act + GELU_CUBE * pre_act * pre_act * pre_act))
    gelu_value = 0.5 * pre_act * (1.0 + tanh_val)
    gelu_slope = 0.5 * (1.0 + tanh_val) + 0.5 * pre_act * (
        1.0 - tanh_val * tanh_val
    ) * GELU_SCALE * (1.0 + 3.0 * GELU_CUBE * pre_act * pre_act)
    return (gelu_value, gelu_slope)


def token_levels(block_order, count_row):
    above_three = count_row[3]
    above_two = above_three + count_row[2]
    above_one = above_two + count_row[1]
    places = jnp.arange(block_order.shape[0], dtype=jnp.int32)
    ranked = (
        (places < above_three).astype(jnp.int32)
        + (places < above_two).astype(jnp.int32)
        + (places < above_one).astype(jnp.int32)
    )
    hits = block_order[None, :] == places[:, None]
    return jnp.sum(jnp.where(hits, ranked[None, :], 0), axis=1)


def column_bands(first_column, column_count, unit_total):
    columns = first_column + jnp.arange(column_count, dtype=jnp.int32)
    return (
        (columns >= unit_total // 8).astype(jnp.int32)
        + (columns >= unit_total // 4).astype(jnp.int32)
        + (columns >= unit_total // 2).astype(jnp.int32)
    )


def norm_backward(grad_normed, standard, row_scale, norm_gain):
    scaled = grad_normed * norm_gain[None, :]
    centre = jnp.mean(scaled, axis=1, keepdims=True)
    along = jnp.mean(scaled * standard, axis=1, keepdims=True)
    return row_scale * (scaled - centre - standard * along)


def shards(inputs, grad_out, norm_gain, level_order, level_counts, weight_in, weight_out):
    rows = inputs.shape[0]
    ring = lax.axis_size("tensor")
    place = lax.axis_index("tensor")
    blocks = lax.axis_size("dp")
    block = lax.axis_index("dp")
    chips = blocks // 2
    unit_local = weight_in.shape[1]
    unit_total = unit_local * ring
    features = inputs.shape[1]
    share = features // blocks

    from_next = [((i + 1) % ring, i) for i in range(ring)]
    from_chip = [((i + 2) % blocks, i) for i in range(blocks)]
    swap_cores = [(i, i ^ 1) for i in range(blocks)]

    as_float = inputs.astype(jnp.float32)
    row_mean = jnp.mean(as_float, axis=1, keepdims=True)
    centred = as_float - row_mean
    row_scale = lax.rsqrt(jnp.mean(centred * centred, axis=1, keepdims=True) + NORM_EPS)
    standard = centred * row_scale
    normed = (standard * norm_gain[None, :]).astype(jnp.bfloat16)

    levels = token_levels(level_order, level_counts[0])
    levels = lax.dynamic_slice_in_dim(jnp.concatenate([levels, levels]), place * rows, rows * ring, 0)
    level_sets = [levels]
    for _ in range(chips - 1):
        level_sets.append(lax.ppermute(level_sets[-1], "dp", from_chip))
    unit_band = column_bands(place * unit_local, unit_local, unit_total)

    own_cols = block * share
    swap_cols = (block ^ 1) * share

    def columns(value, first):
        return lax.dynamic_slice_in_dim(value, first, share, 1)

    grad_ring, normed_ring = grad_out, normed
    hiddens, grad_pres, grad_cols, normed_cols = [], [], [], []
    own_normed_grads = []
    for step in range(ring):
        if step > 0:
            grad_ring = lax.ppermute(grad_ring, "tensor", from_next)
            normed_ring = lax.ppermute(normed_ring, "tensor", from_next)
        grad_set, normed_set = [grad_ring], [normed_ring]
        for _ in range(chips - 1):
            grad_set.append(lax.ppermute(grad_set[-1], "dp", from_chip))
            normed_set.append(lax.ppermute(normed_set[-1], "dp", from_chip))
        grad_rows = jnp.concatenate(grad_set)
        normed_rows = jnp.concatenate(normed_set)
        row_level = jnp.concatenate([one[step * rows : (step + 1) * rows] for one in level_sets])
        unit_mask = unit_band[None, :] <= row_level[:, None]
        pre_act = jnp.dot(normed_rows, weight_in, preferred_element_type=jnp.float32)
        gelu_value, gelu_slope = gelu_parts(pre_act)
        hidden = jnp.where(unit_mask, gelu_value, 0.0).astype(jnp.bfloat16)
        grad_hidden = lax.dot_general(
            grad_rows, weight_out, (((1,), (1,)), ((), ())), preferred_element_type=jnp.float32
        )
        grad_pre = jnp.where(unit_mask, grad_hidden * gelu_slope, 0.0).astype(jnp.bfloat16)
        hiddens += [hidden, lax.ppermute(hidden, "dp", swap_cores)]
        grad_pres += [grad_pre, lax.ppermute(grad_pre, "dp", swap_cores)]
        grad_cols += [
            columns(grad_rows, own_cols),
            lax.ppermute(columns(grad_rows, swap_cols), "dp", swap_cores),
        ]
        normed_cols += [
            columns(normed_rows, own_cols),
            lax.ppermute(columns(normed_rows, swap_cols), "dp", swap_cores),
        ]
        own_normed_grads.append(
            lax.dot_general(
                grad_pre[:rows], weight_in, (((1,), (1,)), ((), ())), preferred_element_type=jnp.float32
            )
        )
    travelling = None
    for step in range(1, ring):
        total = own_normed_grads[step]
        if travelling is not None:
            total = total + travelling.astype(jnp.float32)
        travelling = lax.ppermute(total.astype(jnp.bfloat16), "tensor", from_next)
    own_grad = own_normed_grads[0]
    if travelling is not None:
        own_grad = own_grad + travelling.astype(jnp.float32)
    branch_grad = norm_backward(own_grad, standard, row_scale, norm_gain)
    grad_input = (grad_out.astype(jnp.float32) + branch_grad).astype(jnp.bfloat16)

    grad_weight_out = lax.dot_general(
        jnp.concatenate(hiddens),
        jnp.concatenate(grad_cols),
        (((0,), (0,)), ((), ())),
        preferred_element_type=jnp.float32,
    )
    grad_weight_in = lax.dot_general(
        jnp.concatenate(normed_cols),
        jnp.concatenate(grad_pres),
        (((0,), (0,)), ((), ())),
        preferred_element_type=jnp.float32,
    )
    grad_weight_out = (grad_weight_out / blocks).astype(jnp.bfloat16)
    grad_weight_in = (grad_weight_in / blocks).astype(jnp.bfloat16)
    return (grad_input, grad_weight_in, grad_weight_out)


def solution(mesh):
    in_specs = (
        P(("groups", "dp", "tensor"), None),
        P(("groups", "dp", "tensor"), None),
        P(),
        P(("groups", "dp")),
        P(("groups", "dp"), None),
        P(None, "tensor"),
        P("tensor", None),
    )
    out_specs = (
        P(("groups", "dp", "tensor"), None),
        P(("groups", "dp"), "tensor"),
        P(("groups", "tensor"), "dp"),
    )
    return jax.shard_map(shards, mesh=mesh, in_specs=in_specs, out_specs=out_specs, check_vma=False)
```

```python
import functools

import jax
import jax.numpy as jnp
from jax import lax
from jax.experimental import pallas as pl
from jax.experimental.pallas import tpu as pltpu
from jax.sharding import PartitionSpec as P

GELU_SCALE = 0.7978845608028654
GELU_CUBE = 0.044715
NORM_EPS = 1e-06
GROUP_ROWS = 256
VMEM_LIMIT = 48 * 1024 * 1024


def gelu_parts(pre_act):
    tanh_val = jnp.tanh(GELU_SCALE * (pre_act + GELU_CUBE * pre_act * pre_act * pre_act))
    gelu_value = 0.5 * pre_act * (1.0 + tanh_val)
    gelu_slope = 0.5 * (1.0 + tanh_val) + 0.5 * pre_act * (
        1.0 - tanh_val * tanh_val
    ) * GELU_SCALE * (1.0 + 3.0 * GELU_CUBE * pre_act * pre_act)
    return (gelu_value, gelu_slope)


def token_levels(block_order, count_row):
    above_three = count_row[3]
    above_two = above_three + count_row[2]
    above_one = above_two + count_row[1]
    places = jnp.arange(block_order.shape[0], dtype=jnp.int32)
    ranked = (
        (places < above_three).astype(jnp.int32)
        + (places < above_two).astype(jnp.int32)
        + (places < above_one).astype(jnp.int32)
    )
    hits = block_order[None, :] == places[:, None]
    return jnp.sum(jnp.where(hits, ranked[None, :], 0), axis=1)


def norm_backward(grad_normed, standard, row_scale, norm_gain):
    scaled = grad_normed * norm_gain[None, :]
    centre = jnp.mean(scaled, axis=1, keepdims=True)
    along = jnp.mean(scaled * standard, axis=1, keepdims=True)
    return row_scale * (scaled - centre - standard * along)


def tile_of(extent, wanted):
    while extent % wanted:
        wanted //= 2
    return wanted


def group_kernel(spots, *refs, pieces, unit_total, share, with_grad):
    normed_refs = refs[:pieces]
    grad_refs = refs[pieces : 2 * pieces]
    level_ref, in_ref, out_ref = refs[2 * pieces : 2 * pieces + 3]
    outs = refs[2 * pieces + 3 :]
    acts_ref, own_ref, swap_ref = outs[:3]
    tile = pl.program_id(0)
    normed = jnp.concatenate([ref[...] for ref in normed_refs], axis=0)
    grads = jnp.concatenate([ref[...] for ref in grad_refs], axis=0)

    @pl.when(tile == 0)
    def _():
        own = pl.ds(pl.multiple_of(spots[1], 128), share)
        swap = pl.ds(pl.multiple_of(spots[2], 128), share)
        for kind, sources in enumerate((normed_refs, grad_refs)):
            for at, ref in enumerate(sources):
                size = ref.shape[0]
                own_ref[kind, at * size : (at + 1) * size, :] = ref[:, own]
                swap_ref[kind, at * size : (at + 1) * size, :] = ref[:, swap]

    pre_act = jnp.dot(normed, in_ref[...], preferred_element_type=jnp.float32)
    grad_hidden = lax.dot_general(
        grads, out_ref[...], (((1,), (1,)), ((), ())), preferred_element_type=jnp.float32
    )
    rows, units = pre_act.shape
    column = spots[0] + tile * units + lax.broadcasted_iota(jnp.int32, (rows, units), 1)
    band = (
        (column >= unit_total // 8).astype(jnp.int32)
        + (column >= unit_total // 4).astype(jnp.int32)
        + (column >= unit_total // 2).astype(jnp.int32)
    )
    mask = band <= level_ref[...]
    gelu_value, gelu_slope = gelu_parts(pre_act)
    hidden = jnp.where(mask, gelu_value, 0.0).astype(jnp.bfloat16)
    grad_pre = jnp.where(mask, grad_hidden * gelu_slope, 0.0).astype(jnp.bfloat16)
    acts_ref[0] = grad_pre
    acts_ref[1] = hidden
    if with_grad:
        back_ref = outs[3]
        term = lax.dot_general(
            grad_pre, in_ref[...], (((1,), (1,)), ((), ())), preferred_element_type=jnp.float32
        )

        @pl.when(tile == 0)
        def _():
            back_ref[...] = term

        @pl.when(tile != 0)
        def _():
            back_ref[...] += term


def group_call(spots, normed, grads, level, weight_in, weight_out, unit_total, share, with_grad):
    features, units = weight_in.shape
    pieces = len(normed)
    rows = sum(one.shape[0] for one in normed)
    tile = tile_of(units, 512)
    whole = lambda shape: pl.BlockSpec(shape, lambda i, spots: (0,) * len(shape))
    out_shape = [
        jax.ShapeDtypeStruct((2, rows, units), jnp.bfloat16),
        jax.ShapeDtypeStruct((2, rows, share), jnp.bfloat16),
        jax.ShapeDtypeStruct((2, rows, share), jnp.bfloat16),
    ]
    out_specs = [
        pl.BlockSpec((2, rows, tile), lambda i, spots: (0, 0, i)),
        whole((2, rows, share)),
        whole((2, rows, share)),
    ]
    if with_grad:
        out_shape.append(jax.ShapeDtypeStruct((rows, features), jnp.float32))
        out_specs.append(whole((rows, features)))
    return pl.pallas_call(
        functools.partial(
            group_kernel, pieces=pieces, unit_total=unit_total, share=share, with_grad=with_grad
        ),
        grid_spec=pltpu.PrefetchScalarGridSpec(
            num_scalar_prefetch=1,
            grid=(units // tile,),
            in_specs=[whole(one.shape) for one in (*normed, *grads)]
            + [
                whole((rows, 1)),
                pl.BlockSpec((features, tile), lambda i, spots: (0, i)),
                pl.BlockSpec((tile, features), lambda i, spots: (i, 0)),
            ],
            out_specs=out_specs,
        ),
        out_shape=out_shape,
        compiler_params=pltpu.CompilerParams(vmem_limit_bytes=VMEM_LIMIT),
        cost_estimate=pl.CostEstimate(
            flops=2 * rows * units * features, bytes_accessed=weight_in.size * 2, transcendentals=0
        ),
        name="group",
    )(spots, *normed, *grads, level, weight_in, weight_out)


def weights_kernel(*refs, groups, scale):
    act_refs = refs[:groups]
    col_refs = refs[groups : 2 * groups]
    in_ref, out_ref = refs[2 * groups :]

    def stack(sources, kind):
        return jnp.concatenate([ref[kind] for ref in sources], axis=0)

    def total(left, right):
        return lax.dot_general(
            left, right, (((0,), (0,)), ((), ())), preferred_element_type=jnp.float32
        )

    in_ref[...] = (total(stack(col_refs, 0), stack(act_refs, 0)) * scale).astype(jnp.bfloat16)
    out_ref[...] = (total(stack(act_refs, 1), stack(col_refs, 1)) * scale).astype(jnp.bfloat16)


def weights_call(acts, cols, blocks):
    units, share = acts[0].shape[2], cols[0].shape[2]
    tile = tile_of(units, 512)
    rows = sum(one.shape[1] for one in acts)
    return pl.pallas_call(
        functools.partial(weights_kernel, groups=len(acts), scale=1.0 / blocks),
        grid=(units // tile,),
        in_specs=[pl.BlockSpec((2, one.shape[1], tile), lambda i: (0, 0, i)) for one in acts]
        + [pl.BlockSpec(one.shape, lambda i: (0, 0, 0)) for one in cols],
        out_specs=[
            pl.BlockSpec((share, tile), lambda i: (0, i)),
            pl.BlockSpec((tile, share), lambda i: (i, 0)),
        ],
        out_shape=[
            jax.ShapeDtypeStruct((share, units), jnp.bfloat16),
            jax.ShapeDtypeStruct((units, share), jnp.bfloat16),
        ],
        compiler_params=pltpu.CompilerParams(vmem_limit_bytes=VMEM_LIMIT),
        cost_estimate=pl.CostEstimate(
            flops=4 * rows * units * share, bytes_accessed=2 * rows * units * 2, transcendentals=0
        ),
        name="weights",
    )(*acts, *cols)


def shards(inputs, grad_out, norm_gain, level_order, level_counts, weight_in, weight_out):
    rows = inputs.shape[0]
    ring = lax.axis_size("tensor")
    place = lax.axis_index("tensor")
    blocks = lax.axis_size("dp")
    block = lax.axis_index("dp")
    chips = blocks // 2
    unit_local = weight_in.shape[1]
    unit_total = unit_local * ring
    share = inputs.shape[1] // blocks
    pieces = max(1, min(ring, GROUP_ROWS // rows))

    from_next = [((i + 1) % ring, i) for i in range(ring)]
    from_chip = [((i + 2) % blocks, i) for i in range(blocks)]
    swap_cores = [(i, i ^ 1) for i in range(blocks)]

    as_float = inputs.astype(jnp.float32)
    row_mean = jnp.mean(as_float, axis=1, keepdims=True)
    centred = as_float - row_mean
    row_scale = lax.rsqrt(jnp.mean(centred * centred, axis=1, keepdims=True) + NORM_EPS)
    standard = centred * row_scale
    normed = (standard * norm_gain[None, :]).astype(jnp.bfloat16)

    levels = token_levels(level_order, level_counts[0])
    levels = lax.dynamic_slice_in_dim(jnp.concatenate([levels, levels]), place * rows, rows * ring, 0)
    level_sets = [levels]
    for _ in range(chips - 1):
        level_sets.append(lax.ppermute(level_sets[-1], "dp", from_chip))
    spots = jnp.stack([place * unit_local, block * share, (block ^ 1) * share]).astype(jnp.int32)

    grad_rings, normed_rings = [grad_out], [normed]
    for _ in range(ring - 1):
        grad_rings.append(lax.ppermute(grad_rings[-1], "tensor", from_next))
        normed_rings.append(lax.ppermute(normed_rings[-1], "tensor", from_next))
    grad_sets, normed_sets = [grad_rings], [normed_rings]
    for _ in range(chips - 1):
        grad_sets.append([lax.ppermute(one, "dp", from_chip) for one in grad_sets[-1]])
        normed_sets.append([lax.ppermute(one, "dp", from_chip) for one in normed_sets[-1]])

    acts, cols, own_grads = [], [], []
    for first in range(0, ring, pieces):
        span = slice(first, first + pieces)
        for chip in range(chips):
            level = level_sets[chip][first * rows : (first + pieces) * rows, None]
            act, own_cols, swap_cols, *back = group_call(
                spots,
                normed_sets[chip][span],
                grad_sets[chip][span],
                level,
                weight_in,
                weight_out,
                unit_total,
                share,
                chip == 0,
            )
            acts += [act, lax.ppermute(act, "dp", swap_cores)]
            cols += [own_cols, lax.ppermute(swap_cols, "dp", swap_cores)]
            own_grads += [back[0][i * rows : (i + 1) * rows] for i in range(pieces) if back]
    travelling = None
    for step in range(1, ring):
        total = own_grads[step]
        if travelling is not None:
            total = total + travelling.astype(jnp.float32)
        travelling = lax.ppermute(total.astype(jnp.bfloat16), "tensor", from_next)
    own_grad = own_grads[0]
    if travelling is not None:
        own_grad = own_grad + travelling.astype(jnp.float32)
    branch_grad = norm_backward(own_grad, standard, row_scale, norm_gain)
    grad_input = (grad_out.astype(jnp.float32) + branch_grad).astype(jnp.bfloat16)

    grad_weight_in, grad_weight_out = weights_call(acts, cols, blocks)
    return (grad_input, grad_weight_in, grad_weight_out)


def solution(mesh):
    in_specs = (
        P(("groups", "dp", "tensor"), None),
        P(("groups", "dp", "tensor"), None),
        P(),
        P(("groups", "dp")),
        P(("groups", "dp"), None),
        P(None, "tensor"),
        P("tensor", None),
    )
    out_specs = (
        P(("groups", "dp", "tensor"), None),
        P(("groups", "dp"), "tensor"),
        P(("groups", "tensor"), "dp"),
    )
    return jax.shard_map(shards, mesh=mesh, in_specs=in_specs, out_specs=out_specs, check_vma=False)
```

```python
import functools
import math

import jax
import jax.numpy as jnp
from jax import lax
from jax.experimental import pallas as pl
from jax.experimental.pallas import tpu as pltpu
from jax.sharding import PartitionSpec as P

GELU_SCALE = 0.7978845608028654
GELU_CUBE = 0.044715
NORM_EPS = 1e-06
GROUP_ROWS = 256
VMEM_LIMIT = 48 * 1024 * 1024
WORK = 0.3


def gelu_parts(pre_act):
    square = pre_act * pre_act
    tanh_val = jnp.tanh(pre_act * (GELU_SCALE + (GELU_SCALE * GELU_CUBE) * square))
    share = 0.5 + 0.5 * tanh_val
    gelu_value = pre_act * share
    gelu_slope = share + gelu_value * (1.0 - tanh_val) * (
        GELU_SCALE + (3.0 * GELU_SCALE * GELU_CUBE) * square
    )
    return (gelu_value, gelu_slope)


def token_levels(block_order, count_row):
    above_three = count_row[3]
    above_two = above_three + count_row[2]
    above_one = above_two + count_row[1]
    places = jnp.arange(block_order.shape[0], dtype=jnp.int32)
    ranked = (
        (places < above_three).astype(jnp.int32)
        + (places < above_two).astype(jnp.int32)
        + (places < above_one).astype(jnp.int32)
    )
    hits = block_order[None, :] == places[:, None]
    return jnp.sum(jnp.where(hits, ranked[None, :], 0), axis=1)


def norm_backward(grad_normed, standard, row_scale, norm_gain):
    scaled = grad_normed * norm_gain[None, :]
    centre = jnp.mean(scaled, axis=1, keepdims=True)
    along = jnp.mean(scaled * standard, axis=1, keepdims=True)
    return row_scale * (scaled - centre - standard * along)


def work_of(flops):
    return pl.CostEstimate(flops=int(WORK * flops), bytes_accessed=0, transcendentals=0)


def tile_of(extent, wanted):
    while extent % wanted:
        wanted //= 2
    return wanted


def group_kernel(spots, *refs, pieces, begun, share, with_grad):
    normed_refs = refs[:pieces]
    grad_refs = refs[pieces : 2 * pieces]
    limit_ref, in_ref, out_ref = refs[2 * pieces : 2 * pieces + 3]
    outs = refs[2 * pieces + 3 + begun :]
    acts_ref, own_ref, swap_ref = outs[:3]
    tile = pl.program_id(0)
    normed = jnp.concatenate([ref[...] for ref in normed_refs], axis=0)
    grads = jnp.concatenate([ref[...] for ref in grad_refs], axis=0)

    @pl.when(tile == 0)
    def _():
        own = pl.ds(pl.multiple_of(spots[1], 128), share)
        swap = pl.ds(pl.multiple_of(spots[2], 128), share)
        for kind, parts in enumerate((normed_refs, grad_refs)):
            for at, ref in enumerate(parts):
                size = ref.shape[0]
                own_ref[kind, at * size : (at + 1) * size, :] = ref[:, own]
                swap_ref[kind, at * size : (at + 1) * size, :] = ref[:, swap]

    pre_act = jnp.dot(normed, in_ref[...], preferred_element_type=jnp.float32)
    grad_hidden = lax.dot_general(
        grads, out_ref[...], (((1,), (1,)), ((), ())), preferred_element_type=jnp.float32
    )
    mask = spots[0] + tile * in_ref.shape[1] < limit_ref[...]
    gelu_value, gelu_slope = gelu_parts(pre_act)
    grad_pre = jnp.where(mask, grad_hidden * gelu_slope, 0.0).astype(jnp.bfloat16)
    acts_ref[0] = grad_pre
    acts_ref[1] = jnp.where(mask, gelu_value, 0.0).astype(jnp.bfloat16)
    if with_grad:
        back_refs, total_ref = outs[3:-1], outs[-1]
        term = lax.dot_general(
            grad_pre, in_ref[...], (((1,), (1,)), ((), ())), preferred_element_type=jnp.float32
        )

        @pl.when(tile == 0)
        def _():
            total_ref[...] = term

        @pl.when(tile != 0)
        def _():
            total_ref[...] += term

        @pl.when(tile == pl.num_programs(0) - 1)
        def _():
            for at, ref in enumerate(back_refs):
                size = ref.shape[0]
                ref[...] = total_ref[at * size : (at + 1) * size, :].astype(ref.dtype)


def group_call(
    spots, normed, grads, limit, weight_in, weight_out, tile, share, back_types, chip, chips, begun
):
    features, units = weight_in.shape
    piece_rows = normed[0].shape[0]
    rows = piece_rows * len(normed)
    whole = lambda shape: pl.BlockSpec(shape, lambda i, spots: (0,) * len(shape))
    out_shape = [
        jax.ShapeDtypeStruct((2, chips * rows, units), jnp.bfloat16),
        jax.ShapeDtypeStruct((2, chips * rows, share), jnp.bfloat16),
        jax.ShapeDtypeStruct((2, chips * rows, share), jnp.bfloat16),
    ]
    out_specs = [
        pl.BlockSpec((2, rows, tile), lambda i, spots: (0, chip, i)),
        pl.BlockSpec((2, rows, share), lambda i, spots: (0, chip, 0)),
        pl.BlockSpec((2, rows, share), lambda i, spots: (0, chip, 0)),
    ]
    operands = (spots, *normed, *grads, limit, weight_in, weight_out)
    for kind in back_types:
        out_shape.append(jax.ShapeDtypeStruct((piece_rows, features), kind))
        out_specs.append(whole((piece_rows, features)))
    return pl.pallas_call(
        functools.partial(
            group_kernel,
            pieces=len(normed),
            begun=len(begun),
            share=share,
            with_grad=bool(back_types),
        ),
        grid_spec=pltpu.PrefetchScalarGridSpec(
            num_scalar_prefetch=1,
            grid=(units // tile,),
            in_specs=[whole(one.shape) for one in (*normed, *grads)]
            + [
                whole((rows, 1)),
                pl.BlockSpec((features, tile), lambda i, spots: (0, i)),
                pl.BlockSpec((tile, features), lambda i, spots: (i, 0)),
            ]
            + [pl.BlockSpec(memory_space=pl.ANY) for _ in begun],
            out_specs=out_specs,
            scratch_shapes=[pltpu.VMEM((rows, features), jnp.float32)] if back_types else [],
        ),
        out_shape=out_shape,
        compiler_params=pltpu.CompilerParams(vmem_limit_bytes=VMEM_LIMIT),
        cost_estimate=work_of((6 if back_types else 4) * rows * units * features),
        input_output_aliases={len(operands) + at: at for at in range(len(begun))},
        name="group",
    )(*operands, *begun)


def weights_kernel(*refs, groups, scale, started):
    act_refs = refs[:groups]
    col_refs = refs[groups : 2 * groups]
    in_ref, out_ref = refs[-2:]

    def stack(sources, kind):
        return jnp.concatenate([ref[kind] for ref in sources], axis=0)

    def total(left, right):
        return lax.dot_general(
            left, right, (((0,), (0,)), ((), ())), preferred_element_type=jnp.float32
        )

    for_in = total(stack(col_refs, 0), stack(act_refs, 0))
    for_out = total(stack(act_refs, 1), stack(col_refs, 1))
    if started:
        for_in += refs[-4][...]
        for_out += refs[-3][...]
    in_ref[...] = (for_in * scale).astype(in_ref.dtype)
    out_ref[...] = (for_out * scale).astype(out_ref.dtype)


def weights_call(acts, cols, begun, scale, kind):
    units, share = acts[0].shape[2], cols[0].shape[2]
    tile = tile_of(units, 512)
    in_spec = pl.BlockSpec((share, tile), lambda i: (0, i))
    out_spec = pl.BlockSpec((tile, share), lambda i: (i, 0))
    return pl.pallas_call(
        functools.partial(weights_kernel, groups=len(acts), scale=scale, started=bool(begun)),
        grid=(units // tile,),
        in_specs=[pl.BlockSpec((2, one.shape[1], tile), lambda i: (0, 0, i)) for one in acts]
        + [pl.BlockSpec(one.shape, lambda i: (0, 0, 0)) for one in cols]
        + ([in_spec, out_spec] if begun else []),
        out_specs=[in_spec, out_spec],
        out_shape=[
            jax.ShapeDtypeStruct((share, units), kind),
            jax.ShapeDtypeStruct((units, share), kind),
        ],
        compiler_params=pltpu.CompilerParams(vmem_limit_bytes=VMEM_LIMIT),
        cost_estimate=work_of(4 * sum(one.shape[1] for one in acts) * units * share),
        name="weights",
    )(*acts, *cols, *begun)


def after(value, *others):
    return lax.optimization_barrier((value, others))[0] if others else value


def flat(pairs):
    return [one for pair in pairs for one in pair]


def shards(inputs, grad_out, norm_gain, level_order, level_counts, weight_in, weight_out):
    rows = inputs.shape[0]
    ring = lax.axis_size("tensor")
    place = lax.axis_index("tensor")
    blocks = lax.axis_size("dp")
    block = lax.axis_index("dp")
    chips = blocks // 2
    unit_local = weight_in.shape[1]
    unit_total = unit_local * ring
    share = inputs.shape[1] // blocks
    pieces = max(1, min(ring, GROUP_ROWS // rows))
    tile = tile_of(math.gcd(unit_local, unit_total // 8), 512)

    from_next = [((i + 1) % ring, i) for i in range(ring)]
    from_last = [(i, (i + 1) % ring) for i in range(ring)]
    from_chip = [((i + 2) % blocks, i) for i in range(blocks)]
    swap_cores = [(i, i ^ 1) for i in range(blocks)]
    half = ring // 2

    as_float = inputs.astype(jnp.float32)
    row_mean = jnp.mean(as_float, axis=1, keepdims=True)
    centred = as_float - row_mean
    row_scale = lax.rsqrt(jnp.mean(centred * centred, axis=1, keepdims=True) + NORM_EPS)
    standard = centred * row_scale
    normed = (standard * norm_gain[None, :]).astype(jnp.bfloat16)

    limits = unit_total // (1 << (3 - token_levels(level_order, level_counts[0])))
    limits = lax.dynamic_slice_in_dim(jnp.concatenate([limits, limits]), place * rows, rows * ring, 0)
    limit_sets = [limits]
    for _ in range(chips - 1):
        limit_sets.append(lax.ppermute(limit_sets[-1], "dp", from_chip))
    spots = jnp.stack([place * unit_local, block * share, (block ^ 1) * share]).astype(jnp.int32)

    def send(one, axis, pairs, name):
        with jax.named_scope(name):
            return lax.ppermute(one, axis, pairs)

    kinds = ("grad", "normed")

    def move(piece, axis, pairs, name, *gates):
        return tuple(
            send(after(one, *gates), axis, pairs, f"{name}_{kind}") for one, kind in zip(piece, kinds)
        )

    near = {0: (grad_out, normed)}
    for step in range(1, half + 1):
        near[step] = move(near[step - 1], "tensor", from_next, f"ring_{step}")
    for step in range(ring - 1, half, -1):
        gates = near[1] if step == ring - 1 else ()
        near[step] = move(near[(step + 1) % ring], "tensor", from_last, f"ring_{step}", *gates)
    sets = [[near[step] for step in range(ring)]] + [[None] * ring for _ in range(1, chips)]
    acts, cols, own_grads = [], [], []
    heads = {half, half + 1}

    def over_chips(step, *gates):
        for chip in range(1, chips):
            grads, rows_normed = sets[chip - 1][step]
            grads = send(grads, "dp", from_chip, f"chip_{step}_grad")
            if 0 < step == ring - 1:
                rows_normed = after(sets[chip][0][1], *gates)
                rows_normed = send(rows_normed, "tensor", from_last, f"ring_chip_{step}_normed")
            else:
                rows_normed = send(rows_normed, "dp", from_chip, f"chip_{step}_normed")
            sets[chip][step] = (grads, rows_normed)

    def run_group(first, chip, begun, *gates):
        span = slice(first, first + pieces)
        limit = limit_sets[chip][first * rows : (first + pieces) * rows, None]
        back_types = [
            jnp.bfloat16 if first + i in heads else jnp.float32
            for i in range(pieces if chip == 0 else 0)
        ]
        with jax.named_scope(f"group_{chip}_{first}"):
            act, own_cols, swap_cols, *back = group_call(
                after(spots, *gates),
                [piece[1] for piece in sets[chip][span]],
                [piece[0] for piece in sets[chip][span]],
                limit,
                weight_in,
                weight_out,
                tile,
                share,
                back_types,
                chip,
                chips,
                begun,
            )
        own_grads.extend(back)
        return [act, own_cols, swap_cols]

    def swap(first, results):
        act, own_cols, swap_cols = results
        acts.append([act, send(act, "dp", swap_cores, f"swap_acts_{first}")])
        cols.append([own_cols, send(swap_cols, "dp", swap_cores, f"swap_cols_{first}")])

    for step in range(ring - 1):
        over_chips(step)
    results = run_group(0, 0, [], *[one[0] for one in sets[1:]])
    if ring > 1:
        over_chips(ring - 1, results[2])
    for chip in range(1, chips):
        results = run_group(0, chip, results, *near.get(2, ()))
    swap(0, results)
    totals = []
    for first in range(pieces, ring, pieces):
        gates = []
        if first + pieces >= ring:
            gates = [one[ring - 2][0] for one in sets[1:]]
            totals = weights_call(
                [after(one, *gates) for one in flat(acts)], flat(cols), [], 1.0, jnp.float32
            )
            acts, cols = [], []
            gates = [totals[0]]
        results = []
        for chip in range(chips):
            results = run_group(first, chip, results, *gates)
        swap(first, results)

    def chain(steps, pairs, name):
        travelling = None
        for step in steps:
            total = own_grads[step]
            if travelling is not None:
                total = (total + travelling.astype(jnp.float32)).astype(jnp.bfloat16)
            travelling = send(total.astype(jnp.bfloat16), "tensor", pairs, f"{name}_{step}")
        return travelling

    own_grad = own_grads[0].astype(jnp.float32)
    if ring > 1:
        own_grad = own_grad + chain(range(half, 0, -1), from_last, "sum_up").astype(jnp.float32)
    if ring > 2:
        own_grad = own_grad + chain(range(half + 1, ring), from_next, "sum_down").astype(jnp.float32)
    branch_grad = norm_backward(own_grad, standard, row_scale, norm_gain)
    grad_input = (grad_out.astype(jnp.float32) + branch_grad).astype(jnp.bfloat16)

    grad_weight_in, grad_weight_out = weights_call(
        flat(acts), flat(cols), totals, 1.0 / blocks, jnp.bfloat16
    )
    return (grad_input, grad_weight_in, grad_weight_out)


def solution(mesh):
    in_specs = (
        P(("groups", "dp", "tensor"), None),
        P(("groups", "dp", "tensor"), None),
        P(),
        P(("groups", "dp")),
        P(("groups", "dp"), None),
        P(None, "tensor"),
        P("tensor", None),
    )
    out_specs = (
        P(("groups", "dp", "tensor"), None),
        P(("groups", "dp"), "tensor"),
        P(("groups", "tensor"), "dp"),
    )
    return jax.shard_map(shards, mesh=mesh, in_specs=in_specs, out_specs=out_specs, check_vma=False)
```

```python
import functools
import math

import jax
import jax.numpy as jnp
from jax import lax
from jax.experimental import pallas as pl
from jax.experimental.pallas import tpu as pltpu
from jax.sharding import PartitionSpec as P

GELU_SCALE = 0.7978845608028654
GELU_CUBE = 0.044715
NORM_EPS = 1e-06
VMEM_LIMIT = 48 * 1024 * 1024
WORK = 4.0


def gelu_parts(pre_act):
    square = pre_act * pre_act
    tanh_val = jnp.tanh(pre_act * (GELU_SCALE + (GELU_SCALE * GELU_CUBE) * square))
    share = 0.5 + 0.5 * tanh_val
    gelu_value = pre_act * share
    gelu_slope = share + gelu_value * (1.0 - tanh_val) * (
        GELU_SCALE + (3.0 * GELU_SCALE * GELU_CUBE) * square
    )
    return (gelu_value, gelu_slope)


def token_levels(block_order, count_row):
    above_three = count_row[3]
    above_two = above_three + count_row[2]
    above_one = above_two + count_row[1]
    places = jnp.arange(block_order.shape[0], dtype=jnp.int32)
    ranked = (
        (places < above_three).astype(jnp.int32)
        + (places < above_two).astype(jnp.int32)
        + (places < above_one).astype(jnp.int32)
    )
    hits = block_order[None, :] == places[:, None]
    return jnp.sum(jnp.where(hits, ranked[None, :], 0), axis=1)


def norm_backward(grad_normed, standard, row_scale, norm_gain):
    scaled = grad_normed * norm_gain[None, :]
    centre = jnp.mean(scaled, axis=1, keepdims=True)
    along = jnp.mean(scaled * standard, axis=1, keepdims=True)
    return row_scale * (scaled - centre - standard * along)


def work_of(flops):
    return pl.CostEstimate(flops=int(WORK * flops), bytes_accessed=0, transcendentals=0)


def tile_of(extent, wanted):
    while extent % wanted:
        wanted //= 2
    return wanted


def group_kernel(spots, *refs, pieces, owned, share, tiles):
    normed_refs = refs[:pieces]
    grad_refs = refs[pieces : 2 * pieces]
    limit_ref, in_ref, out_ref = refs[2 * pieces : 2 * pieces + 3]
    acts_ref, own_ref = refs[2 * pieces + 3 : 2 * pieces + 5]
    rest = refs[2 * pieces + 5 :]
    tile = pl.program_id(0)

    def columns(target, first):
        span = pl.ds(pl.multiple_of(first, 128), share)
        for kind, sources in enumerate((normed_refs, grad_refs)):
            for at, ref in enumerate(sources):
                size = ref.shape[0]
                target[kind, at * size : (at + 1) * size, :] = ref[:, span]

    @pl.when(tile == 0)
    def _():
        columns(own_ref, spots[1])

    @pl.when(tile == tiles)
    def _():
        columns(acts_ref, spots[2])

    @pl.when(tile < tiles)
    def _():
        group_tile(spots[0], normed_refs, grad_refs, limit_ref, in_ref, out_ref, acts_ref, rest, owned, tiles)


def group_tile(first, normed_refs, grad_refs, limit_ref, in_ref, out_ref, acts_ref, rest, owned, tiles):
    tile = pl.program_id(0)
    units = in_ref.shape[1]
    width = 256 if units % 256 == 0 else units
    normed = jnp.concatenate([ref[...] for ref in normed_refs], axis=0)
    grads = jnp.concatenate([ref[...] for ref in grad_refs], axis=0)

    mask = first + tile * units < limit_ref[...]
    products = []
    for start in range(0, units, width):
        span = slice(start, start + width)
        pre_act = jnp.dot(normed, in_ref[:, span], preferred_element_type=jnp.float32)
        grad_hidden = lax.dot_general(
            grads, out_ref[span, :], (((1,), (1,)), ((), ())), preferred_element_type=jnp.float32
        )
        products.append((span, pre_act, grad_hidden))
    for span, pre_act, grad_hidden in products:
        gelu_value, gelu_slope = gelu_parts(pre_act)
        acts_ref[0, :, span] = jnp.where(mask, grad_hidden * gelu_slope, 0.0).astype(jnp.bfloat16)
        acts_ref[1, :, span] = jnp.where(mask, gelu_value, 0.0).astype(jnp.bfloat16)
    if owned:
        back_refs, total_ref = rest[:-1], rest[-1]
        term = lax.dot_general(
            acts_ref[0, : total_ref.shape[0], :],
            in_ref[...],
            (((1,), (1,)), ((), ())),
            preferred_element_type=jnp.float32,
        )

        @pl.when(tile == 0)
        def _():
            total_ref[...] = term

        @pl.when(tile != 0)
        def _():
            total_ref[...] += term

        @pl.when(tile == tiles - 1)
        def _():
            for at, ref in enumerate(back_refs):
                size = ref.shape[0]
                ref[...] = total_ref[at * size : (at + 1) * size, :].astype(ref.dtype)


def group_call(spots, normed, grads, limit, weight_in, weight_out, tile, share, back_types):
    features, units = weight_in.shape
    piece_rows = normed[0].shape[0]
    rows = piece_rows * len(normed)
    owned = len(back_types)
    tiles = units // tile
    whole = lambda shape: pl.BlockSpec(shape, lambda i, spots: (0,) * len(shape))
    out_shape = [
        jax.ShapeDtypeStruct((2, rows, units + share), jnp.bfloat16),
        jax.ShapeDtypeStruct((2, rows, share), jnp.bfloat16),
    ]
    out_specs = [
        pl.BlockSpec((2, rows, tile), lambda i, spots: (0, 0, i)),
        whole((2, rows, share)),
    ]
    for kind in back_types:
        out_shape.append(jax.ShapeDtypeStruct((piece_rows, features), kind))
        out_specs.append(whole((piece_rows, features)))
    return pl.pallas_call(
        functools.partial(
            group_kernel, pieces=len(normed), owned=owned, share=share, tiles=tiles
        ),
        grid_spec=pltpu.PrefetchScalarGridSpec(
            num_scalar_prefetch=1,
            grid=(tiles + share // tile,),
            in_specs=[whole(one.shape) for one in (*normed, *grads)]
            + [
                whole((rows, 1)),
                pl.BlockSpec((features, tile), lambda i, spots: (0, jnp.minimum(i, tiles - 1))),
                pl.BlockSpec((tile, features), lambda i, spots: (jnp.minimum(i, tiles - 1), 0)),
            ],
            out_specs=out_specs,
            scratch_shapes=[pltpu.VMEM((owned * piece_rows, features), jnp.float32)] if owned else [],
        ),
        out_shape=out_shape,
        compiler_params=pltpu.CompilerParams(vmem_limit_bytes=VMEM_LIMIT),
        cost_estimate=work_of((4 * rows + 2 * owned * piece_rows) * units * features),
        name="group",
    )(spots, *normed, *grads, limit, weight_in, weight_out)


def weights_kernel(*refs, groups, scale, started):
    act_refs = refs[:groups]
    col_refs = refs[groups : 2 * groups]
    in_ref, out_ref = refs[-2:]

    def stack(sources, kind):
        return jnp.concatenate([ref[kind] for ref in sources], axis=0)

    def total(left, right):
        return lax.dot_general(
            left, right, (((0,), (0,)), ((), ())), preferred_element_type=jnp.float32
        )

    for_in = total(stack(col_refs, 0), stack(act_refs, 0))
    for_out = total(stack(act_refs, 1), stack(col_refs, 1))
    if started:
        for_in += refs[-4][...].astype(jnp.float32)
        for_out += refs[-3][...].astype(jnp.float32)
    in_ref[...] = (for_in * scale).astype(in_ref.dtype)
    out_ref[...] = (for_out * scale).astype(out_ref.dtype)


def weights_call(groups, begun, scale):
    share = groups[0][1].shape[2]
    units = groups[0][0].shape[2] - share
    tile = tile_of(units, 512)
    acts, acts_specs, cols, cols_specs = [], [], [], []
    for own, own_cols, other in groups:
        rows = own.shape[1]
        acts += [own, other]
        acts_specs += [pl.BlockSpec((2, rows, tile), lambda i: (0, 0, i))] * 2
        cols += [own_cols, other]
        cols_specs += [
            pl.BlockSpec((2, rows, share), lambda i: (0, 0, 0)),
            pl.BlockSpec((2, rows, share), lambda i: (0, 0, units // share)),
        ]
    in_spec = pl.BlockSpec((share, tile), lambda i: (0, i))
    out_spec = pl.BlockSpec((tile, share), lambda i: (i, 0))
    return pl.pallas_call(
        functools.partial(weights_kernel, groups=len(acts), scale=scale, started=bool(begun)),
        grid=(units // tile,),
        in_specs=acts_specs + cols_specs + ([in_spec, out_spec] if begun else []),
        out_specs=[in_spec, out_spec],
        out_shape=[
            jax.ShapeDtypeStruct((share, units), jnp.bfloat16),
            jax.ShapeDtypeStruct((units, share), jnp.bfloat16),
        ],
        compiler_params=pltpu.CompilerParams(vmem_limit_bytes=VMEM_LIMIT),
        cost_estimate=work_of(4 * sum(one.shape[1] for one in acts) * units * share),
        name="weights",
    )(*acts, *cols, *begun)


def after(value, *others):
    return lax.optimization_barrier((value, others))[0] if others else value


def shards(inputs, grad_out, norm_gain, level_order, level_counts, weight_in, weight_out):
    rows = inputs.shape[0]
    ring = lax.axis_size("tensor")
    place = lax.axis_index("tensor")
    blocks = lax.axis_size("dp")
    block = lax.axis_index("dp")
    chips = blocks // 2
    unit_local = weight_in.shape[1]
    unit_total = unit_local * ring
    share = inputs.shape[1] // blocks
    tile = math.gcd(unit_local, unit_total // 8, share)

    from_next = [((i + 1) % ring, i) for i in range(ring)]
    from_last = [(i, (i + 1) % ring) for i in range(ring)]
    from_chip = [((i + 2) % blocks, i) for i in range(blocks)]
    swap_cores = [(i, i ^ 1) for i in range(blocks)]
    half = ring // 2

    as_float = inputs.astype(jnp.float32)
    row_mean = jnp.mean(as_float, axis=1, keepdims=True)
    centred = as_float - row_mean
    row_scale = lax.rsqrt(jnp.mean(centred * centred, axis=1, keepdims=True) + NORM_EPS)
    standard = centred * row_scale
    normed = (standard * norm_gain[None, :]).astype(jnp.bfloat16)

    def limits_of(order, counts):
        limits = unit_total // (1 << (3 - token_levels(order, counts)))
        limits = jnp.concatenate([limits, limits])
        return lax.dynamic_slice_in_dim(limits, place * rows, rows * ring, 0)

    spots = jnp.stack([place * unit_local, block * share, (block ^ 1) * share]).astype(jnp.int32)

    def send(one, axis, pairs, name):
        with jax.named_scope(name):
            return lax.ppermute(one, axis, pairs)

    kinds = ("grad", "normed")

    def move(piece, axis, pairs, name, *gates):
        return tuple(
            send(after(one, *gates), axis, pairs, f"{name}_{kind}") for one, kind in zip(piece, kinds)
        )

    near = {0: (grad_out, normed)}
    for step in range(1, ring):
        near[step] = move(near[step - 1], "tensor", from_next, f"ring_{step}")
    sets = [[near[step] for step in range(ring)]]
    limit_sets = [limits_of(level_order, level_counts[0])]
    levels = jnp.concatenate([level_order, level_counts[0]])
    for chip in range(1, chips):
        levels = send(levels, "dp", from_chip, "chip_levels")
        limit_sets.append(limits_of(levels[:-4], levels[-4:]))
        far = []
        for step, (grads, rows_normed) in enumerate(sets[-1]):
            grads = send(grads, "dp", from_chip, f"chip_{step}_grad")
            if step == 0:
                rows_normed = after(rows_normed, levels)
            far.append((grads, send(rows_normed, "dp", from_chip, f"chip_{step}_normed")))
        sets.append(far)

    groups, own_grads = [], []
    arrivals = [
        [(chip, slot - chip) for chip in range(chips) if 0 <= slot - chip < ring]
        for slot in range(ring + chips - 1)
    ]
    if len(arrivals) > 1:
        arrivals[:2] = [sorted(arrivals[0] + arrivals[1])]
    totals = []
    for at, entries in enumerate(arrivals):
        gates = []
        if at > 0 and at == len(arrivals) - 1:
            early = [sets[chip][step][0] for chip, step in entries]
            totals = weights_call(
                [(after(own, *early), *others) for own, *others in groups[:-1]], [], 1.0
            )
            gates = [totals[0]]
            groups = groups[-1:]
        own_steps = [step for chip, step in entries if chip == 0]
        back_types = [jnp.bfloat16 if step in (half, half + 1) else jnp.float32 for step in own_steps]
        limit = jnp.concatenate(
            [limit_sets[chip][step * rows : (step + 1) * rows, None] for chip, step in entries]
        )
        with jax.named_scope(f"group_{at}"):
            act, own_cols, *back = group_call(
                after(spots, *gates),
                [sets[chip][step][1] for chip, step in entries],
                [sets[chip][step][0] for chip, step in entries],
                limit,
                weight_in,
                weight_out,
                tile,
                share,
                back_types,
            )
        own_grads.extend(back)
        groups.append((act, own_cols, send(act, "dp", swap_cores, f"swap_{at}")))

    def chain(steps, pairs, name):
        travelling = None
        for step in steps:
            total = own_grads[step]
            if travelling is not None:
                total = (total + travelling.astype(jnp.float32)).astype(jnp.bfloat16)
            travelling = send(total.astype(jnp.bfloat16), "tensor", pairs, f"{name}_{step}")
        return travelling

    own_grad = own_grads[0].astype(jnp.float32)
    if ring > 1:
        own_grad = own_grad + chain(range(half, 0, -1), from_last, "sum_up").astype(jnp.float32)
    if ring > 2:
        own_grad = own_grad + chain(range(half + 1, ring), from_next, "sum_down").astype(jnp.float32)
    branch_grad = norm_backward(own_grad, standard, row_scale, norm_gain)
    grad_input = (grad_out.astype(jnp.float32) + branch_grad).astype(jnp.bfloat16)

    grad_weight_in, grad_weight_out = weights_call(groups, totals, 1.0 / blocks)
    return (grad_input, grad_weight_in, grad_weight_out)


def solution(mesh):
    in_specs = (
        P(("groups", "dp", "tensor"), None),
        P(("groups", "dp", "tensor"), None),
        P(),
        P(("groups", "dp")),
        P(("groups", "dp"), None),
        P(None, "tensor"),
        P("tensor", None),
    )
    out_specs = (
        P(("groups", "dp", "tensor"), None),
        P(("groups", "dp"), "tensor"),
        P(("groups", "tensor"), "dp"),
    )
    return jax.shard_map(shards, mesh=mesh, in_specs=in_specs, out_specs=out_specs, check_vma=False)
```

```python
import functools
import math

import jax
import jax.numpy as jnp
from jax import lax
from jax.experimental import pallas as pl
from jax.experimental.pallas import tpu as pltpu
from jax.sharding import PartitionSpec as P

GELU_SCALE = 0.7978845608028654
GELU_CUBE = 0.044715
NORM_EPS = 1e-06
VMEM_LIMIT = 48 * 1024 * 1024
WORK = 3.0
WEIGHTS = {2: 3.0}


def gelu_parts(pre_act):
    square = pre_act * pre_act
    tanh_val = jnp.tanh(pre_act * (GELU_SCALE + (GELU_SCALE * GELU_CUBE) * square))
    share = 0.5 + 0.5 * tanh_val
    gelu_value = pre_act * share
    gelu_slope = share + gelu_value * (1.0 - tanh_val) * (
        GELU_SCALE + (3.0 * GELU_SCALE * GELU_CUBE) * square
    )
    return (gelu_value, gelu_slope)


def token_levels(block_order, count_row):
    above_three = count_row[3]
    above_two = above_three + count_row[2]
    above_one = above_two + count_row[1]
    places = jnp.arange(block_order.shape[0], dtype=jnp.int32)
    ranked = (
        (places < above_three).astype(jnp.int32)
        + (places < above_two).astype(jnp.int32)
        + (places < above_one).astype(jnp.int32)
    )
    hits = block_order[None, :] == places[:, None]
    return jnp.sum(jnp.where(hits, ranked[None, :], 0), axis=1)


def norm_backward(grad_normed, standard, row_scale, norm_gain):
    scaled = grad_normed * norm_gain[None, :]
    centre = jnp.mean(scaled, axis=1, keepdims=True)
    along = jnp.mean(scaled * standard, axis=1, keepdims=True)
    return row_scale * (scaled - centre - standard * along)


def work_of(flops):
    return pl.CostEstimate(flops=int(WORK * flops), bytes_accessed=0, transcendentals=0)


def tile_of(extent, wanted):
    while extent % wanted:
        wanted //= 2
    return wanted


def group_kernel(spots, *refs, pieces, begun, owned, share, tiles):
    normed_refs = refs[:pieces]
    grad_refs = refs[pieces : 2 * pieces]
    limit_ref, in_ref, out_ref = refs[2 * pieces : 2 * pieces + 3]
    acts_ref, own_ref, *rest = refs[2 * pieces + 3 + begun :]
    tile = pl.program_id(0)

    def columns(target, first):
        span = pl.ds(pl.multiple_of(first, 128), share)
        for kind, sources in enumerate((normed_refs, grad_refs)):
            for at, ref in enumerate(sources):
                size = ref.shape[0]
                target[kind, at * size : (at + 1) * size, :] = ref[:, span]

    rows_ref, rest = rest[-1], rest[:-1]

    @pl.when(tile == 0)
    def _():
        columns(own_ref, spots[1])
        for kind, sources in enumerate((normed_refs, grad_refs)):
            for at, ref in enumerate(sources):
                size = ref.shape[0]
                rows_ref[kind, at * size : (at + 1) * size, :] = ref[...]

    @pl.when(tile == tiles)
    def _():
        columns(acts_ref, spots[2])

    @pl.when(tile < tiles)
    def _():
        group_tile(spots[0], rows_ref, limit_ref, in_ref, out_ref, acts_ref, rest, owned, tiles)


def group_tile(first, rows_ref, limit_ref, in_ref, out_ref, acts_ref, rest, owned, tiles):
    tile = pl.program_id(0)
    units = in_ref.shape[1]
    width = 256 if units % 256 == 0 else units

    mask = first + tile * units < limit_ref[...]
    products = []
    for start in range(0, units, width):
        span = slice(start, start + width)
        pre_act = jnp.dot(rows_ref[0], in_ref[:, span], preferred_element_type=jnp.float32)
        grad_hidden = lax.dot_general(
            rows_ref[1], out_ref[span, :], (((1,), (1,)), ((), ())), preferred_element_type=jnp.float32
        )
        products.append((span, pre_act, grad_hidden))
    for span, pre_act, grad_hidden in products:
        gelu_value, gelu_slope = gelu_parts(pre_act)
        acts_ref[0, :, span] = jnp.where(mask, grad_hidden * gelu_slope, 0.0).astype(jnp.bfloat16)
        acts_ref[1, :, span] = jnp.where(mask, gelu_value, 0.0).astype(jnp.bfloat16)
    if owned:
        back_refs, total_ref = rest[:-1], rest[-1]
        term = lax.dot_general(
            acts_ref[0, : total_ref.shape[0], :],
            in_ref[...],
            (((1,), (1,)), ((), ())),
            preferred_element_type=jnp.float32,
        )

        @pl.when(tile == 0)
        def _():
            total_ref[...] = term

        @pl.when(tile != 0)
        def _():
            total_ref[...] += term

        @pl.when(tile == tiles - 1)
        def _():
            for at, ref in enumerate(back_refs):
                size = ref.shape[0]
                ref[...] = total_ref[at * size : (at + 1) * size, :].astype(ref.dtype)


def group_call(
    spots, normed, grads, limit, weight_in, weight_out, tile, share, back_types, begun, rows_after, weight
):
    features, units = weight_in.shape
    piece_rows = normed[0].shape[0]
    rows = piece_rows * len(normed)
    owned = len(back_types)
    tiles = units // tile
    total = begun[0].shape[1] if begun else rows + rows_after
    whole = lambda shape: pl.BlockSpec(shape, lambda i, spots: (0,) * len(shape))
    out_shape = [
        jax.ShapeDtypeStruct((2, total, units + share), jnp.bfloat16),
        jax.ShapeDtypeStruct((2, total, share), jnp.bfloat16),
    ]
    out_specs = [
        pl.BlockSpec((2, rows, tile), lambda i, spots: (0, rows_after // rows, i)),
        pl.BlockSpec((2, rows, share), lambda i, spots: (0, rows_after // rows, 0)),
    ]
    operands = (spots, *normed, *grads, limit, weight_in, weight_out)
    for kind in back_types:
        out_shape.append(jax.ShapeDtypeStruct((piece_rows, features), kind))
        out_specs.append(whole((piece_rows, features)))
    return pl.pallas_call(
        functools.partial(
            group_kernel,
            pieces=len(normed),
            begun=len(begun),
            owned=owned,
            share=share,
            tiles=tiles,
        ),
        grid_spec=pltpu.PrefetchScalarGridSpec(
            num_scalar_prefetch=1,
            grid=(tiles + share // tile,),
            in_specs=[whole(one.shape) for one in (*normed, *grads)]
            + [
                whole((rows, 1)),
                pl.BlockSpec((features, tile), lambda i, spots: (0, jnp.minimum(i, tiles - 1))),
                pl.BlockSpec((tile, features), lambda i, spots: (jnp.minimum(i, tiles - 1), 0)),
            ]
            + [pl.BlockSpec(memory_space=pl.ANY) for _ in begun],
            out_specs=out_specs,
            scratch_shapes=[pltpu.VMEM((owned * piece_rows, features), jnp.float32)] * bool(owned)
            + [pltpu.VMEM((2, rows, features), jnp.bfloat16)],
        ),
        out_shape=out_shape,
        compiler_params=pltpu.CompilerParams(vmem_limit_bytes=VMEM_LIMIT),
        cost_estimate=work_of(weight * (4 * rows + 2 * owned * piece_rows) * units * features),
        input_output_aliases={len(operands) + at: at for at in range(len(begun))},
        name="group",
    )(*operands, *begun)


def weights_kernel(*refs, groups, scale, started):
    act_refs = refs[:groups]
    col_refs = refs[groups : 2 * groups]
    in_ref, out_ref = refs[-2:]

    def stack(sources, kind):
        return jnp.concatenate([ref[kind] for ref in sources], axis=0)

    def total(left, right):
        return lax.dot_general(
            left, right, (((0,), (0,)), ((), ())), preferred_element_type=jnp.float32
        )

    for_in = total(stack(col_refs, 0), stack(act_refs, 0))
    for_out = total(stack(act_refs, 1), stack(col_refs, 1))
    if started:
        for_in += refs[-4][...].astype(jnp.float32)
        for_out += refs[-3][...].astype(jnp.float32)
    in_ref[...] = (for_in * scale).astype(in_ref.dtype)
    out_ref[...] = (for_out * scale).astype(out_ref.dtype)


def weights_call(groups, begun, scale):
    share = groups[0][1].shape[2]
    units = groups[0][0].shape[2] - share
    tile = tile_of(units, 512)
    acts, acts_specs, cols, cols_specs = [], [], [], []
    for own, own_cols, other in groups:
        rows = own.shape[1]
        acts += [own, other]
        acts_specs += [pl.BlockSpec((2, rows, tile), lambda i: (0, 0, i))] * 2
        cols += [own_cols, other]
        cols_specs += [
            pl.BlockSpec((2, rows, share), lambda i: (0, 0, 0)),
            pl.BlockSpec((2, rows, share), lambda i: (0, 0, units // share)),
        ]
    in_spec = pl.BlockSpec((share, tile), lambda i: (0, i))
    out_spec = pl.BlockSpec((tile, share), lambda i: (i, 0))
    return pl.pallas_call(
        functools.partial(weights_kernel, groups=len(acts), scale=scale, started=bool(begun)),
        grid=(units // tile,),
        in_specs=acts_specs + cols_specs + ([in_spec, out_spec] if begun else []),
        out_specs=[in_spec, out_spec],
        out_shape=[
            jax.ShapeDtypeStruct((share, units), jnp.bfloat16),
            jax.ShapeDtypeStruct((units, share), jnp.bfloat16),
        ],
        compiler_params=pltpu.CompilerParams(vmem_limit_bytes=VMEM_LIMIT),
        cost_estimate=work_of(0),
        name="weights",
    )(*acts, *cols, *begun)


def after(value, *others):
    return lax.optimization_barrier((value, others))[0] if others else value


def shards(inputs, grad_out, norm_gain, level_order, level_counts, weight_in, weight_out):
    rows = inputs.shape[0]
    ring = lax.axis_size("tensor")
    place = lax.axis_index("tensor")
    blocks = lax.axis_size("dp")
    block = lax.axis_index("dp")
    chips = blocks // 2
    unit_local = weight_in.shape[1]
    unit_total = unit_local * ring
    share = inputs.shape[1] // blocks
    tile = math.gcd(unit_local, unit_total // 8, share)

    from_next = [((i + 1) % ring, i) for i in range(ring)]
    from_last = [(i, (i + 1) % ring) for i in range(ring)]
    from_chip = [((i + 2) % blocks, i) for i in range(blocks)]
    swap_cores = [(i, i ^ 1) for i in range(blocks)]
    half = ring // 2

    as_float = inputs.astype(jnp.float32)
    row_mean = jnp.mean(as_float, axis=1, keepdims=True)
    centred = as_float - row_mean
    row_scale = lax.rsqrt(jnp.mean(centred * centred, axis=1, keepdims=True) + NORM_EPS)
    standard = centred * row_scale
    normed = (standard * norm_gain[None, :]).astype(jnp.bfloat16)

    def limits_of(order, counts):
        limits = unit_total // (1 << (3 - token_levels(order, counts)))
        limits = jnp.concatenate([limits, limits])
        return lax.dynamic_slice_in_dim(limits, place * rows, rows * ring, 0)

    spots = jnp.stack([place * unit_local, block * share, (block ^ 1) * share]).astype(jnp.int32)

    def send(one, axis, pairs, name):
        with jax.named_scope(name):
            return lax.ppermute(one, axis, pairs)

    kinds = ("normed", "grad")

    def move(piece, axis, pairs, name, *gates):
        return tuple(
            send(after(one, *gates), axis, pairs, f"{name}_{kind}") for one, kind in zip(piece, kinds)
        )

    near = {0: (normed, grad_out)}
    for step in range(1, ring):
        near[step] = move(near[step - 1], "tensor", from_next, f"ring_{step}")
    sets = [[near[step] for step in range(ring)]]
    limit_sets = [limits_of(level_order, level_counts[0])]
    levels = jnp.concatenate([level_order, level_counts[0]])

    for chip in range(1, chips):
        levels = send(levels, "dp", from_chip, "chip_levels")
        limit_sets.append(limits_of(levels[:-4], levels[-4:]))
        far = []
        for step, piece in enumerate(sets[-1]):
            held = [levels] if step == 0 else []
            far.append(move(piece, "dp", from_chip, f"chip_{step}", *held))
        sets.append(far)

    groups, own_grads = [], []
    arrivals = [
        [(chip, slot - chip) for chip in range(chips) if 0 <= slot - chip < ring]
        for slot in range(ring + chips - 1)
    ]
    last = len(arrivals) - 1
    totals = []
    for at, entries in enumerate(arrivals):
        gates, begun, rows_after = [], [], 0
        if at == 0 and last > 0:
            rows_after = rows * len(arrivals[1])
        elif at == 1:
            begun = groups.pop()[:2]
        if last > 2 and at >= last - 1:
            early = [sets[chip][step][1] for chip, step in entries]
            totals = weights_call(
                [(after(own, *early), *others) for own, *others in groups[:-1]], totals, 1.0
            )
            gates = [totals[0]]
            groups = groups[-1:]
        own_steps = [step for chip, step in entries if chip == 0]
        back_types = [jnp.bfloat16 if step in (half, half + 1) else jnp.float32 for step in own_steps]
        limit = jnp.concatenate(
            [limit_sets[chip][step * rows : (step + 1) * rows, None] for chip, step in entries]
        )
        with jax.named_scope(f"group_{at}"):
            act, own_cols, *back = group_call(
                after(spots, *gates),
                [sets[chip][step][0] for chip, step in entries],
                [sets[chip][step][1] for chip, step in entries],
                limit,
                weight_in,
                weight_out,
                tile,
                share,
                back_types,
                begun,
                rows_after,
                WEIGHTS.get(at, 1.0),
            )
        own_grads.extend(back)
        if at == 0 and last > 0:
            groups.append((act, own_cols))
        else:
            groups.append((act, own_cols, send(act, "dp", swap_cores, f"swap_{at}")))

    def chain(steps, pairs, name):
        travelling = None
        for step in steps:
            total = own_grads[step]
            if travelling is not None:
                total = (total + travelling.astype(jnp.float32)).astype(jnp.bfloat16)
            travelling = send(total.astype(jnp.bfloat16), "tensor", pairs, f"{name}_{step}")
        return travelling

    own_grad = own_grads[0].astype(jnp.float32)
    if ring > 1:
        own_grad = own_grad + chain(range(half, 0, -1), from_last, "sum_up").astype(jnp.float32)
    if ring > 2:
        own_grad = own_grad + chain(range(half + 1, ring), from_next, "sum_down").astype(jnp.float32)
    branch_grad = norm_backward(own_grad, standard, row_scale, norm_gain)
    grad_input = (grad_out.astype(jnp.float32) + branch_grad).astype(jnp.bfloat16)

    grad_weight_in, grad_weight_out = weights_call(groups, totals, 1.0 / blocks)
    return (grad_input, grad_weight_in, grad_weight_out)


def solution(mesh):
    in_specs = (
        P(("groups", "dp", "tensor"), None),
        P(("groups", "dp", "tensor"), None),
        P(),
        P(("groups", "dp")),
        P(("groups", "dp"), None),
        P(None, "tensor"),
        P("tensor", None),
    )
    out_specs = (
        P(("groups", "dp", "tensor"), None),
        P(("groups", "dp"), "tensor"),
        P(("groups", "tensor"), "dp"),
    )
    return jax.shard_map(shards, mesh=mesh, in_specs=in_specs, out_specs=out_specs, check_vma=False)
```

```python
import functools
import math

import jax
import jax.numpy as jnp
from jax import lax
from jax.experimental import pallas as pl
from jax.experimental.pallas import tpu as pltpu
from jax.sharding import PartitionSpec as P

GELU_SCALE = 0.7978845608028654
GELU_CUBE = 0.044715
NORM_EPS = 1e-06
VMEM_LIMIT = 48 * 1024 * 1024
WORK = 3.0
WEIGHTS = {1: 3.0}


def gelu_parts(pre_act):
    square = pre_act * pre_act
    tanh_val = jnp.tanh(pre_act * (GELU_SCALE + (GELU_SCALE * GELU_CUBE) * square))
    share = 0.5 + 0.5 * tanh_val
    gelu_value = pre_act * share
    gelu_slope = share + gelu_value * (1.0 - tanh_val) * (
        GELU_SCALE + (3.0 * GELU_SCALE * GELU_CUBE) * square
    )
    return (gelu_value, gelu_slope)


def unit_limits(block_order, count_row, first, unit_total):
    above_three = count_row[3]
    above_two = above_three + count_row[2]
    above_one = above_two + count_row[1]
    count = block_order.shape[0]
    places = jnp.arange(count, dtype=jnp.int32)
    ranked = (
        (places < above_three).astype(jnp.int32)
        + (places < above_two).astype(jnp.int32)
        + (places < above_one).astype(jnp.int32)
    )
    tokens = (first + places) % count
    hits = block_order[None, :] == tokens[:, None]
    limits = unit_total // (1 << (3 - ranked))
    return jnp.sum(jnp.where(hits, limits[None, :], 0), axis=1, keepdims=True)


def norm_backward(grad_normed, standard, row_scale, norm_gain):
    scaled = grad_normed * norm_gain[None, :]
    centre = jnp.mean(scaled, axis=1, keepdims=True)
    along = jnp.mean(scaled * standard, axis=1, keepdims=True)
    return row_scale * (scaled - centre - standard * along)


def work_of(flops):
    return pl.CostEstimate(flops=int(WORK * flops), bytes_accessed=0, transcendentals=0)


def tile_of(extent, wanted):
    while extent % wanted:
        wanted //= 2
    return wanted


def group_kernel(spots, *refs, limit_at, owned, share, tiles):
    pieces, sets = len(limit_at), 1 + max(at for at, _ in limit_at)
    normed_refs = refs[:pieces]
    grad_refs = refs[pieces : 2 * pieces]
    limit_refs = refs[2 * pieces : 2 * pieces + sets]
    in_ref, out_ref, acts_ref, own_ref, *rest = refs[2 * pieces + sets :]
    tile = pl.program_id(0)

    def columns(target, first):
        span = pl.ds(pl.multiple_of(first, 128), share)
        for kind, sources in enumerate((normed_refs, grad_refs)):
            for at, ref in enumerate(sources):
                size = ref.shape[0]
                target[kind, at * size : (at + 1) * size, :] = ref[:, span]

    rows_ref, rest = rest[-1], rest[:-1]
    size = normed_refs[0].shape[0]
    limit = jnp.concatenate([limit_refs[at][step * size : (step + 1) * size, :] for at, step in limit_at])

    @pl.when(tile == 0)
    def _():
        columns(own_ref, spots[1])
        for kind, sources in enumerate((normed_refs, grad_refs)):
            for at, ref in enumerate(sources):
                size = ref.shape[0]
                rows_ref[kind, at * size : (at + 1) * size, :] = ref[...]

    @pl.when(tile == tiles)
    def _():
        columns(acts_ref, spots[2])

    @pl.when(tile < tiles)
    def _():
        group_tile(spots[0], rows_ref, limit, in_ref, out_ref, acts_ref, rest, owned, tiles)


def group_tile(first, rows_ref, limit, in_ref, out_ref, acts_ref, rest, owned, tiles):
    tile = pl.program_id(0)
    units = in_ref.shape[1]
    width = 256 if units % 256 == 0 else units

    mask = first + tile * units < limit
    products = []
    for start in range(0, units, width):
        span = slice(start, start + width)
        pre_act = jnp.dot(rows_ref[0], in_ref[:, span], preferred_element_type=jnp.float32)
        grad_hidden = lax.dot_general(
            rows_ref[1], out_ref[span, :], (((1,), (1,)), ((), ())), preferred_element_type=jnp.float32
        )
        products.append((span, pre_act, grad_hidden))
    for span, pre_act, grad_hidden in products:
        gelu_value, gelu_slope = gelu_parts(pre_act)
        acts_ref[0, :, span] = jnp.where(mask, grad_hidden * gelu_slope, 0.0).astype(jnp.bfloat16)
        acts_ref[1, :, span] = jnp.where(mask, gelu_value, 0.0).astype(jnp.bfloat16)
    if owned:
        back_refs, total_ref = rest[:-1], rest[-1]
        term = lax.dot_general(
            acts_ref[0, : total_ref.shape[0], :],
            in_ref[...],
            (((1,), (1,)), ((), ())),
            preferred_element_type=jnp.float32,
        )

        @pl.when(tile == 0)
        def _():
            total_ref[...] = term

        @pl.when(tile != 0)
        def _():
            total_ref[...] += term

        @pl.when(tile == tiles - 1)
        def _():
            for at, ref in enumerate(back_refs):
                size = ref.shape[0]
                ref[...] = total_ref[at * size : (at + 1) * size, :].astype(ref.dtype)


def group_call(
    spots, normed, grads, limits, limit_at, weight_in, weight_out, tile, share, back_types, weight
):
    features, units = weight_in.shape
    piece_rows = normed[0].shape[0]
    rows = piece_rows * len(normed)
    owned = len(back_types)
    tiles = units // tile
    whole = lambda shape: pl.BlockSpec(shape, lambda i, spots: (0,) * len(shape))
    out_shape = [
        jax.ShapeDtypeStruct((2, rows, units + share), jnp.bfloat16),
        jax.ShapeDtypeStruct((2, rows, share), jnp.bfloat16),
    ]
    out_specs = [
        pl.BlockSpec((2, rows, tile), lambda i, spots: (0, 0, i)),
        whole((2, rows, share)),
    ]
    for kind in back_types:
        out_shape.append(jax.ShapeDtypeStruct((piece_rows, features), kind))
        out_specs.append(whole((piece_rows, features)))
    return pl.pallas_call(
        functools.partial(
            group_kernel, limit_at=limit_at, owned=owned, share=share, tiles=tiles
        ),
        grid_spec=pltpu.PrefetchScalarGridSpec(
            num_scalar_prefetch=1,
            grid=(tiles + share // tile,),
            in_specs=[whole(one.shape) for one in (*normed, *grads, *limits)]
            + [
                pl.BlockSpec((features, tile), lambda i, spots: (0, jnp.minimum(i, tiles - 1))),
                pl.BlockSpec((tile, features), lambda i, spots: (jnp.minimum(i, tiles - 1), 0)),
            ],
            out_specs=out_specs,
            scratch_shapes=[pltpu.VMEM((owned * piece_rows, features), jnp.float32)] * bool(owned)
            + [pltpu.VMEM((2, rows, features), jnp.bfloat16)],
        ),
        out_shape=out_shape,
        compiler_params=pltpu.CompilerParams(vmem_limit_bytes=VMEM_LIMIT),
        cost_estimate=work_of(weight * (4 * rows + 2 * owned * piece_rows) * units * features),
        name="group",
    )(spots, *normed, *grads, *limits, weight_in, weight_out)


def weights_kernel(*refs, groups, scale, started):
    act_refs = refs[:groups]
    col_refs = refs[groups : 2 * groups]
    in_ref, out_ref = refs[-2:]

    def stack(sources, kind):
        return jnp.concatenate([ref[kind] for ref in sources], axis=0)

    def total(left, right):
        return lax.dot_general(
            left, right, (((0,), (0,)), ((), ())), preferred_element_type=jnp.float32
        )

    for_in = total(stack(col_refs, 0), stack(act_refs, 0))
    for_out = total(stack(act_refs, 1), stack(col_refs, 1))
    if started:
        for_in += refs[-4][...].astype(jnp.float32)
        for_out += refs[-3][...].astype(jnp.float32)
    in_ref[...] = (for_in * scale).astype(in_ref.dtype)
    out_ref[...] = (for_out * scale).astype(out_ref.dtype)


def weights_call(groups, begun, scale):
    share = groups[0][1].shape[2]
    units = groups[0][0].shape[2] - share
    tile = tile_of(units, 512)
    acts, acts_specs, cols, cols_specs = [], [], [], []
    for own, own_cols, other in groups:
        rows = own.shape[1]
        acts += [own, other]
        acts_specs += [pl.BlockSpec((2, rows, tile), lambda i: (0, 0, i))] * 2
        cols += [own_cols, other]
        cols_specs += [
            pl.BlockSpec((2, rows, share), lambda i: (0, 0, 0)),
            pl.BlockSpec((2, rows, share), lambda i: (0, 0, units // share)),
        ]
    in_spec = pl.BlockSpec((share, tile), lambda i: (0, i))
    out_spec = pl.BlockSpec((tile, share), lambda i: (i, 0))
    return pl.pallas_call(
        functools.partial(weights_kernel, groups=len(acts), scale=scale, started=bool(begun)),
        grid=(units // tile,),
        in_specs=acts_specs + cols_specs + ([in_spec, out_spec] if begun else []),
        out_specs=[in_spec, out_spec],
        out_shape=[
            jax.ShapeDtypeStruct((share, units), jnp.bfloat16),
            jax.ShapeDtypeStruct((units, share), jnp.bfloat16),
        ],
        compiler_params=pltpu.CompilerParams(vmem_limit_bytes=VMEM_LIMIT),
        cost_estimate=work_of(0),
        name="weights",
    )(*acts, *cols, *begun)


def after(value, *others):
    return lax.optimization_barrier((value, others))[0] if others else value


def shards(inputs, grad_out, norm_gain, level_order, level_counts, weight_in, weight_out):
    rows = inputs.shape[0]
    ring = lax.axis_size("tensor")
    place = lax.axis_index("tensor")
    blocks = lax.axis_size("dp")
    block = lax.axis_index("dp")
    chips = blocks // 2
    unit_local = weight_in.shape[1]
    unit_total = unit_local * ring
    share = inputs.shape[1] // blocks
    tile = math.gcd(unit_local, unit_total // 8, share)

    from_next = [((i + 1) % ring, i) for i in range(ring)]
    from_last = [(i, (i + 1) % ring) for i in range(ring)]
    from_chip = [((i + 2) % blocks, i) for i in range(blocks)]
    swap_cores = [(i, i ^ 1) for i in range(blocks)]
    half = ring // 2

    def send(one, axis, pairs, name):
        with jax.named_scope(name):
            return lax.ppermute(one, axis, pairs)

    level_sets = [jnp.concatenate([level_order, level_counts[0]])]
    for _ in range(1, chips):
        level_sets.append(send(level_sets[-1], "dp", from_chip, "chip_levels"))

    as_float = after(inputs, *level_sets[1:]).astype(jnp.float32)
    row_mean = jnp.mean(as_float, axis=1, keepdims=True)
    centred = as_float - row_mean
    row_scale = lax.rsqrt(jnp.mean(centred * centred, axis=1, keepdims=True) + NORM_EPS)
    standard = centred * row_scale
    normed = (standard * norm_gain[None, :]).astype(jnp.bfloat16)

    limits = [unit_limits(one[:-4], one[-4:], place * rows, unit_total) for one in level_sets]
    spots = jnp.stack([place * unit_local, block * share, (block ^ 1) * share]).astype(jnp.int32)

    kinds = ("normed", "grad")

    def move(piece, axis, pairs, name, *gates):
        return tuple(
            send(after(one, *gates), axis, pairs, f"{name}_{kind}") for one, kind in zip(piece, kinds)
        )

    near = {0: (normed, grad_out)}
    for step in range(1, ring):
        near[step] = move(near[step - 1], "tensor", from_next, f"ring_{step}")
    sets = [[near[step] for step in range(ring)]]
    for chip in range(1, chips):
        sets.append(
            [move(piece, "dp", from_chip, f"chip_{step}") for step, piece in enumerate(sets[-1])]
        )

    groups, own_grads = [], []
    arrivals = [
        [(chip, slot - chip) for chip in range(chips) if 0 <= slot - chip < ring]
        for slot in range(ring + chips - 1)
    ]
    if len(arrivals) > 1:
        arrivals[:2] = [sorted(arrivals[0] + arrivals[1])]
    last = len(arrivals) - 1
    totals = []
    for at, entries in enumerate(arrivals):
        gates = []
        if last > 1 and at >= last - 1:
            early = [sets[chip][step][1] for chip, step in entries]
            totals = weights_call(
                [(after(own, *early), *others) for own, *others in groups[:-1]], totals, 1.0
            )
            gates = [totals[0]]
            groups = groups[-1:]
        own_steps = [step for chip, step in entries if chip == 0]
        back_types = [jnp.bfloat16 if step in (half, half + 1) else jnp.float32 for step in own_steps]
        with jax.named_scope(f"group_{at}"):
            act, own_cols, *back = group_call(
                after(spots, *gates),
                [sets[chip][step][0] for chip, step in entries],
                [sets[chip][step][1] for chip, step in entries],
                limits[: 1 + max(chip for chip, _ in entries)],
                entries,
                weight_in,
                weight_out,
                tile,
                share,
                back_types,
                WEIGHTS.get(at, 1.0),
            )
        own_grads.extend(back)
        groups.append((act, own_cols, send(act, "dp", swap_cores, f"swap_{at}")))

    def chain(steps, pairs, name):
        travelling = None
        for step in steps:
            total = own_grads[step]
            if travelling is not None:
                total = (total + travelling.astype(jnp.float32)).astype(jnp.bfloat16)
            travelling = send(total.astype(jnp.bfloat16), "tensor", pairs, f"{name}_{step}")
        return travelling

    own_grad = own_grads[0].astype(jnp.float32)
    if ring > 1:
        own_grad = own_grad + chain(range(half, 0, -1), from_last, "sum_up").astype(jnp.float32)
    if ring > 2:
        own_grad = own_grad + chain(range(half + 1, ring), from_next, "sum_down").astype(jnp.float32)
    branch_grad = norm_backward(own_grad, standard, row_scale, norm_gain)
    grad_input = (grad_out.astype(jnp.float32) + branch_grad).astype(jnp.bfloat16)

    grad_weight_in, grad_weight_out = weights_call(groups, totals, 1.0 / blocks)
    return (grad_input, grad_weight_in, grad_weight_out)


def solution(mesh):
    in_specs = (
        P(("groups", "dp", "tensor"), None),
        P(("groups", "dp", "tensor"), None),
        P(),
        P(("groups", "dp")),
        P(("groups", "dp"), None),
        P(None, "tensor"),
        P("tensor", None),
    )
    out_specs = (
        P(("groups", "dp", "tensor"), None),
        P(("groups", "dp"), "tensor"),
        P(("groups", "tensor"), "dp"),
    )
    return jax.shard_map(shards, mesh=mesh, in_specs=in_specs, out_specs=out_specs, check_vma=False)
```

```python
import functools
import math

import jax
import jax.numpy as jnp
from jax import lax
from jax.experimental import pallas as pl
from jax.experimental.pallas import tpu as pltpu
from jax.sharding import PartitionSpec as P

GELU_SCALE = 0.7978845608028654
GELU_CUBE = 0.044715
NORM_EPS = 1e-06
VMEM_LIMIT = 48 * 1024 * 1024
WORK = 3.0
WEIGHTS = {1: 3.0}


def gelu_parts(pre_act):
    square = pre_act * pre_act
    tanh_val = jnp.tanh(pre_act * (GELU_SCALE + (GELU_SCALE * GELU_CUBE) * square))
    share = 0.5 + 0.5 * tanh_val
    gelu_value = pre_act * share
    gelu_slope = share + gelu_value * (1.0 - tanh_val) * (
        GELU_SCALE + (3.0 * GELU_SCALE * GELU_CUBE) * square
    )
    return (gelu_value, gelu_slope)


def unit_limits(block_order, count_row, first, unit_total):
    above_three = count_row[3]
    above_two = above_three + count_row[2]
    above_one = above_two + count_row[1]
    count = block_order.shape[0]
    places = jnp.arange(count, dtype=jnp.int32)
    ranked = (
        (places < above_three).astype(jnp.int32)
        + (places < above_two).astype(jnp.int32)
        + (places < above_one).astype(jnp.int32)
    )
    tokens = (first + places) % count
    hits = block_order[None, :] == tokens[:, None]
    limits = unit_total // (1 << (3 - ranked))
    return jnp.sum(jnp.where(hits, limits[None, :], 0), axis=1, keepdims=True)


def norm_backward(grad_normed, standard, row_scale, norm_gain):
    scaled = grad_normed * norm_gain[None, :]
    centre = jnp.mean(scaled, axis=1, keepdims=True)
    along = jnp.mean(scaled * standard, axis=1, keepdims=True)
    return row_scale * (scaled - centre - standard * along)


def work_of(flops):
    return pl.CostEstimate(flops=int(WORK * flops), bytes_accessed=0, transcendentals=0)


def tile_of(extent, wanted):
    while extent % wanted:
        wanted //= 2
    return wanted


def group_kernel(spots, *refs, limit_at, owned, share, tiles):
    pieces, sets = len(limit_at), 1 + max(at for at, _ in limit_at)
    normed_refs = refs[:pieces]
    grad_refs = refs[pieces : 2 * pieces]
    limit_refs = refs[2 * pieces : 2 * pieces + sets]
    in_ref, out_ref, acts_ref, own_ref, *rest = refs[2 * pieces + sets :]
    tile = pl.program_id(0)

    def columns(target, first):
        span = pl.ds(pl.multiple_of(first, 128), share)
        for kind, sources in enumerate((normed_refs, grad_refs)):
            for at, ref in enumerate(sources):
                size = ref.shape[0]
                target[kind, at * size : (at + 1) * size, :] = ref[:, span]

    rows_ref, rest = rest[-1], rest[:-1]
    size = normed_refs[0].shape[0]
    limit = jnp.concatenate([limit_refs[at][step * size : (step + 1) * size, :] for at, step in limit_at])

    @pl.when(tile == 0)
    def _():
        columns(own_ref, spots[1])
        for kind, sources in enumerate((normed_refs, grad_refs)):
            for at, ref in enumerate(sources):
                size = ref.shape[0]
                rows_ref[kind, at * size : (at + 1) * size, :] = ref[...]

    @pl.when(tile == tiles)
    def _():
        columns(acts_ref, spots[2])

    @pl.when(tile < tiles)
    def _():
        group_tile(spots[0], rows_ref, limit, in_ref, out_ref, acts_ref, rest, owned, tiles)


def group_tile(first, rows_ref, limit, in_ref, out_ref, acts_ref, rest, owned, tiles):
    tile = pl.program_id(0)
    units = in_ref.shape[1]
    width = 256 if units % 256 == 0 else units

    mask = first + tile * units < limit
    products = []
    for start in range(0, units, width):
        span = slice(start, start + width)
        pre_act = jnp.dot(rows_ref[0], in_ref[:, span], preferred_element_type=jnp.float32)
        grad_hidden = lax.dot_general(
            rows_ref[1], out_ref[span, :], (((1,), (1,)), ((), ())), preferred_element_type=jnp.float32
        )
        products.append((span, pre_act, grad_hidden))
    for span, pre_act, grad_hidden in products:
        gelu_value, gelu_slope = gelu_parts(pre_act)
        acts_ref[0, :, span] = jnp.where(mask, grad_hidden * gelu_slope, 0.0).astype(jnp.bfloat16)
        acts_ref[1, :, span] = jnp.where(mask, gelu_value, 0.0).astype(jnp.bfloat16)
    if owned:
        back_refs, total_ref = rest[:-1], rest[-1]
        term = lax.dot_general(
            acts_ref[0, : total_ref.shape[0], :],
            in_ref[...],
            (((1,), (1,)), ((), ())),
            preferred_element_type=jnp.float32,
        )

        @pl.when(tile == 0)
        def _():
            total_ref[...] = term

        @pl.when(tile != 0)
        def _():
            total_ref[...] += term

        @pl.when(tile == tiles - 1)
        def _():
            for at, ref in enumerate(back_refs):
                size = ref.shape[0]
                ref[...] = total_ref[at * size : (at + 1) * size, :].astype(ref.dtype)


def group_call(
    spots, normed, grads, limits, limit_at, weight_in, weight_out, tile, share, back_types, weight
):
    features, units = weight_in.shape
    piece_rows = normed[0].shape[0]
    rows = piece_rows * len(normed)
    owned = len(back_types)
    tiles = units // tile
    whole = lambda shape: pl.BlockSpec(shape, lambda i, spots: (0,) * len(shape))
    out_shape = [
        jax.ShapeDtypeStruct((2, rows, units + share), jnp.bfloat16),
        jax.ShapeDtypeStruct((2, rows, share), jnp.bfloat16),
    ]
    out_specs = [
        pl.BlockSpec((2, rows, tile), lambda i, spots: (0, 0, i)),
        whole((2, rows, share)),
    ]
    for kind in back_types:
        out_shape.append(jax.ShapeDtypeStruct((piece_rows, features), kind))
        out_specs.append(whole((piece_rows, features)))
    return pl.pallas_call(
        functools.partial(
            group_kernel, limit_at=limit_at, owned=owned, share=share, tiles=tiles
        ),
        grid_spec=pltpu.PrefetchScalarGridSpec(
            num_scalar_prefetch=1,
            grid=(tiles + share // tile,),
            in_specs=[whole(one.shape) for one in (*normed, *grads, *limits)]
            + [
                pl.BlockSpec((features, tile), lambda i, spots: (0, jnp.minimum(i, tiles - 1))),
                pl.BlockSpec((tile, features), lambda i, spots: (jnp.minimum(i, tiles - 1), 0)),
            ],
            out_specs=out_specs,
            scratch_shapes=[pltpu.VMEM((owned * piece_rows, features), jnp.float32)] * bool(owned)
            + [pltpu.VMEM((2, rows, features), jnp.bfloat16)],
        ),
        out_shape=out_shape,
        compiler_params=pltpu.CompilerParams(vmem_limit_bytes=VMEM_LIMIT),
        cost_estimate=work_of(weight * (4 * rows + 2 * owned * piece_rows) * units * features),
        name="group",
    )(spots, *normed, *grads, *limits, weight_in, weight_out)


def weights_kernel(*refs, groups, scale, started):
    act_refs = refs[:groups]
    col_refs = refs[groups : 2 * groups]
    in_ref, out_ref = refs[-2:]

    def stack(sources, kind):
        return jnp.concatenate([ref[kind] for ref in sources], axis=0)

    def total(left, right):
        return lax.dot_general(
            left, right, (((0,), (0,)), ((), ())), preferred_element_type=jnp.float32
        )

    for_in = total(stack(col_refs, 0), stack(act_refs, 0))
    for_out = total(stack(act_refs, 1), stack(col_refs, 1))
    if started:
        for_in += refs[-4][...].astype(jnp.float32)
        for_out += refs[-3][...].astype(jnp.float32)
    in_ref[...] = (for_in * scale).astype(in_ref.dtype)
    out_ref[...] = (for_out * scale).astype(out_ref.dtype)


def weights_call(groups, begun, scale):
    share = groups[0][1].shape[2]
    units = groups[0][0].shape[2] - share
    tile = tile_of(units, 512)
    acts, acts_specs, cols, cols_specs = [], [], [], []
    for own, own_cols, other in groups:
        rows = own.shape[1]
        acts += [own, other]
        acts_specs += [pl.BlockSpec((2, rows, tile), lambda i: (0, 0, i))] * 2
        cols += [own_cols, other]
        cols_specs += [
            pl.BlockSpec((2, rows, share), lambda i: (0, 0, 0)),
            pl.BlockSpec((2, rows, share), lambda i: (0, 0, units // share)),
        ]
    in_spec = pl.BlockSpec((share, tile), lambda i: (0, i))
    out_spec = pl.BlockSpec((tile, share), lambda i: (i, 0))
    return pl.pallas_call(
        functools.partial(weights_kernel, groups=len(acts), scale=scale, started=bool(begun)),
        grid=(units // tile,),
        in_specs=acts_specs + cols_specs + ([in_spec, out_spec] if begun else []),
        out_specs=[in_spec, out_spec],
        out_shape=[
            jax.ShapeDtypeStruct((share, units), jnp.bfloat16),
            jax.ShapeDtypeStruct((units, share), jnp.bfloat16),
        ],
        compiler_params=pltpu.CompilerParams(vmem_limit_bytes=VMEM_LIMIT),
        cost_estimate=work_of(0),
        name="weights",
    )(*acts, *cols, *begun)


def after(value, *others):
    return lax.optimization_barrier((value, others))[0] if others else value


def shards(inputs, grad_out, norm_gain, level_order, level_counts, weight_in, weight_out):
    rows = inputs.shape[0]
    ring = lax.axis_size("tensor")
    place = lax.axis_index("tensor")
    blocks = lax.axis_size("dp")
    block = lax.axis_index("dp")
    chips = blocks // 2
    unit_local = weight_in.shape[1]
    unit_total = unit_local * ring
    share = inputs.shape[1] // blocks
    tile = math.gcd(unit_local, unit_total // 8, share)

    from_next = [((i + 1) % ring, i) for i in range(ring)]
    from_last = [(i, (i + 1) % ring) for i in range(ring)]
    from_chip = [((i + 2) % blocks, i) for i in range(blocks)]
    swap_cores = [(i, i ^ 1) for i in range(blocks)]
    half = ring // 2

    def send(one, axis, pairs, name):
        with jax.named_scope(name):
            return lax.ppermute(one, axis, pairs)

    level_sets = [jnp.concatenate([level_order, level_counts[0]])]
    for _ in range(1, chips):
        level_sets.append(send(level_sets[-1], "dp", from_chip, "chip_levels"))

    as_float = after(inputs, *level_sets[1:]).astype(jnp.float32)
    row_mean = jnp.mean(as_float, axis=1, keepdims=True)
    centred = as_float - row_mean
    row_scale = lax.rsqrt(jnp.mean(centred * centred, axis=1, keepdims=True) + NORM_EPS)
    standard = centred * row_scale
    normed = (standard * norm_gain[None, :]).astype(jnp.bfloat16)

    limits = [unit_limits(one[:-4], one[-4:], place * rows, unit_total) for one in level_sets]
    spots = jnp.stack([place * unit_local, block * share, (block ^ 1) * share]).astype(jnp.int32)

    kinds = ("normed", "grad")

    def move(piece, axis, pairs, name, *gates):
        return tuple(
            send(after(one, *gates), axis, pairs, f"{name}_{kind}") for one, kind in zip(piece, kinds)
        )

    near = {0: (normed, grad_out)}
    for step in range(1, ring):
        near[step] = move(near[step - 1], "tensor", from_next, f"ring_{step}")
    sets = [[near[step] for step in range(ring)]]
    for chip in range(1, chips):
        sets.append(
            [
                None if step == ring - 1 else move(piece, "dp", from_chip, f"chip_{step}")
                for step, piece in enumerate(sets[-1])
            ]
        )

    def last_over_chips(*gates):
        for chip in range(1, chips):
            normed_rows, grads = sets[chip - 1][-1]
            name = f"chip_{ring - 1}"
            grads = send(after(grads, *gates), "dp", from_chip, f"{name}_grad")
            normed_rows = send(after(normed_rows, *gates), "dp", from_chip, f"{name}_normed")
            sets[chip][-1] = (normed_rows, grads)

    groups, own_grads = [], []
    arrivals = [
        [(chip, slot - chip) for chip in range(chips) if 0 <= slot - chip < ring]
        for slot in range(ring + chips - 1)
    ]
    if len(arrivals) > 1:
        arrivals[:2] = [sorted(arrivals[0] + arrivals[1])]
    last = len(arrivals) - 1
    totals, hold = [], []
    for at, entries in enumerate(arrivals):
        gates = []
        if any(sets[chip][step] is None for chip, step in entries):
            last_over_chips(*hold)
        if last > 1 and at >= last - 1:
            early = [sets[chip][step][1] for chip, step in entries] if hold else []
            totals = weights_call(
                [(after(own, *early), *others) for own, *others in groups[:-1]], totals, 1.0
            )
            gates = [totals[0]]
            hold = hold or gates
            groups = groups[-1:]
        own_steps = [step for chip, step in entries if chip == 0]
        back_types = [jnp.bfloat16 if step in (half, half + 1) else jnp.float32 for step in own_steps]
        with jax.named_scope(f"group_{at}"):
            act, own_cols, *back = group_call(
                after(spots, *gates),
                [sets[chip][step][0] for chip, step in entries],
                [sets[chip][step][1] for chip, step in entries],
                limits[: 1 + max(chip for chip, _ in entries)],
                entries,
                weight_in,
                weight_out,
                tile,
                share,
                back_types,
                WEIGHTS.get(at, 1.0),
            )
        own_grads.extend(back)
        groups.append((act, own_cols, send(act, "dp", swap_cores, f"swap_{at}")))

    def chain(steps, pairs, name):
        travelling = None
        for step in steps:
            total = after(own_grads[step], *hold)
            if travelling is not None:
                total = (total + travelling.astype(jnp.float32)).astype(jnp.bfloat16)
            travelling = send(total.astype(jnp.bfloat16), "tensor", pairs, f"{name}_{step}")
        return travelling

    own_grad = own_grads[0].astype(jnp.float32)
    if ring > 1:
        own_grad = own_grad + chain(range(half, 0, -1), from_last, "sum_up").astype(jnp.float32)
    if ring > 2:
        own_grad = own_grad + chain(range(half + 1, ring), from_next, "sum_down").astype(jnp.float32)
    branch_grad = norm_backward(own_grad, standard, row_scale, norm_gain)
    grad_input = (grad_out.astype(jnp.float32) + branch_grad).astype(jnp.bfloat16)

    grad_weight_in, grad_weight_out = weights_call(groups, totals, 1.0 / blocks)
    return (grad_input, grad_weight_in, grad_weight_out)


def solution(mesh):
    in_specs = (
        P(("groups", "dp", "tensor"), None),
        P(("groups", "dp", "tensor"), None),
        P(),
        P(("groups", "dp")),
        P(("groups", "dp"), None),
        P(None, "tensor"),
        P("tensor", None),
    )
    out_specs = (
        P(("groups", "dp", "tensor"), None),
        P(("groups", "dp"), "tensor"),
        P(("groups", "tensor"), "dp"),
    )
    return jax.shard_map(shards, mesh=mesh, in_specs=in_specs, out_specs=out_specs, check_vma=False)
```

```python
import functools
import math

import jax
import jax.numpy as jnp
from jax import lax
from jax.experimental import pallas as pl
from jax.experimental.pallas import tpu as pltpu
from jax.sharding import PartitionSpec as P

GELU_SCALE = 0.7978845608028654
GELU_CUBE = 0.044715
NORM_EPS = 1e-06
VMEM_LIMIT = 48 * 1024 * 1024
WORK = 3.0
WEIGHTS = {1: 3.0, 3: 3.0}


def gelu_parts(pre_act):
    square = pre_act * pre_act
    tanh_val = jnp.tanh(pre_act * (GELU_SCALE + (GELU_SCALE * GELU_CUBE) * square))
    share = 0.5 + 0.5 * tanh_val
    gelu_value = pre_act * share
    gelu_slope = share + gelu_value * (1.0 - tanh_val) * (
        GELU_SCALE + (3.0 * GELU_SCALE * GELU_CUBE) * square
    )
    return (gelu_value, gelu_slope)


def unit_limits(block_order, count_row, first, unit_total):
    above_three = count_row[3]
    above_two = above_three + count_row[2]
    above_one = above_two + count_row[1]
    count = block_order.shape[0]
    places = jnp.arange(count, dtype=jnp.int32)
    ranked = (
        (places < above_three).astype(jnp.int32)
        + (places < above_two).astype(jnp.int32)
        + (places < above_one).astype(jnp.int32)
    )
    tokens = (first + places) % count
    hits = block_order[None, :] == tokens[:, None]
    limits = unit_total // (1 << (3 - ranked))
    return jnp.sum(jnp.where(hits, limits[None, :], 0), axis=1, keepdims=True)


def norm_backward(grad_normed, standard, row_scale, norm_gain):
    scaled = grad_normed * norm_gain[None, :]
    centre = jnp.mean(scaled, axis=1, keepdims=True)
    along = jnp.mean(scaled * standard, axis=1, keepdims=True)
    return row_scale * (scaled - centre - standard * along)


def work_of(flops):
    return pl.CostEstimate(flops=int(WORK * flops), bytes_accessed=0, transcendentals=0)


def tile_of(extent, wanted):
    while extent % wanted:
        wanted //= 2
    return wanted


def group_kernel(spots, *refs, limit_at, owned, share, tiles):
    pieces, sets = len(limit_at), 1 + max(at for at, _ in limit_at)
    normed_refs = refs[:pieces]
    grad_refs = refs[pieces : 2 * pieces]
    limit_refs = refs[2 * pieces : 2 * pieces + sets]
    in_ref, out_ref, acts_ref, own_ref, *rest = refs[2 * pieces + sets :]
    tile = pl.program_id(0)

    def columns(target, first):
        span = pl.ds(pl.multiple_of(first, 128), share)
        for kind, sources in enumerate((normed_refs, grad_refs)):
            for at, ref in enumerate(sources):
                size = ref.shape[0]
                target[kind, at * size : (at + 1) * size, :] = ref[:, span]

    rows_ref, rest = rest[-1], rest[:-1]
    size = normed_refs[0].shape[0]
    limit = jnp.concatenate([limit_refs[at][step * size : (step + 1) * size, :] for at, step in limit_at])

    @pl.when(tile == 0)
    def _():
        columns(own_ref, spots[1])
        for kind, sources in enumerate((normed_refs, grad_refs)):
            for at, ref in enumerate(sources):
                size = ref.shape[0]
                rows_ref[kind, at * size : (at + 1) * size, :] = ref[...]

    @pl.when(tile == tiles)
    def _():
        columns(acts_ref, spots[2])

    @pl.when(tile < tiles)
    def _():
        group_tile(spots[0], rows_ref, limit, in_ref, out_ref, acts_ref, rest, owned, tiles)


def group_tile(first, rows_ref, limit, in_ref, out_ref, acts_ref, rest, owned, tiles):
    tile = pl.program_id(0)
    units = in_ref.shape[1]
    width = 256 if units % 256 == 0 else units

    mask = first + tile * units < limit
    products = []
    for start in range(0, units, width):
        span = slice(start, start + width)
        pre_act = jnp.dot(rows_ref[0], in_ref[:, span], preferred_element_type=jnp.float32)
        grad_hidden = lax.dot_general(
            rows_ref[1], out_ref[span, :], (((1,), (1,)), ((), ())), preferred_element_type=jnp.float32
        )
        products.append((span, pre_act, grad_hidden))
    for span, pre_act, grad_hidden in products:
        gelu_value, gelu_slope = gelu_parts(pre_act)
        acts_ref[0, :, span] = jnp.where(mask, grad_hidden * gelu_slope, 0.0).astype(jnp.bfloat16)
        acts_ref[1, :, span] = jnp.where(mask, gelu_value, 0.0).astype(jnp.bfloat16)
    if owned:
        back_refs, total_ref = rest[:-1], rest[-1]
        term = lax.dot_general(
            acts_ref[0, : total_ref.shape[0], :],
            in_ref[...],
            (((1,), (1,)), ((), ())),
            preferred_element_type=jnp.float32,
        )

        @pl.when(tile == 0)
        def _():
            total_ref[...] = term

        @pl.when(tile != 0)
        def _():
            total_ref[...] += term

        @pl.when(tile == tiles - 1)
        def _():
            for at, ref in enumerate(back_refs):
                size = ref.shape[0]
                ref[...] = total_ref[at * size : (at + 1) * size, :].astype(ref.dtype)


def group_call(
    spots, normed, grads, limits, limit_at, weight_in, weight_out, tile, share, back_types, weight
):
    features, units = weight_in.shape
    piece_rows = normed[0].shape[0]
    rows = piece_rows * len(normed)
    owned = len(back_types)
    tiles = units // tile
    whole = lambda shape: pl.BlockSpec(shape, lambda i, spots: (0,) * len(shape))
    out_shape = [
        jax.ShapeDtypeStruct((2, rows, units + share), jnp.bfloat16),
        jax.ShapeDtypeStruct((2, rows, share), jnp.bfloat16),
    ]
    out_specs = [
        pl.BlockSpec((2, rows, tile), lambda i, spots: (0, 0, i)),
        whole((2, rows, share)),
    ]
    for kind in back_types:
        out_shape.append(jax.ShapeDtypeStruct((piece_rows, features), kind))
        out_specs.append(whole((piece_rows, features)))
    return pl.pallas_call(
        functools.partial(
            group_kernel, limit_at=limit_at, owned=owned, share=share, tiles=tiles
        ),
        grid_spec=pltpu.PrefetchScalarGridSpec(
            num_scalar_prefetch=1,
            grid=(tiles + share // tile,),
            in_specs=[whole(one.shape) for one in (*normed, *grads, *limits)]
            + [
                pl.BlockSpec((features, tile), lambda i, spots: (0, jnp.minimum(i, tiles - 1))),
                pl.BlockSpec((tile, features), lambda i, spots: (jnp.minimum(i, tiles - 1), 0)),
            ],
            out_specs=out_specs,
            scratch_shapes=[pltpu.VMEM((owned * piece_rows, features), jnp.float32)] * bool(owned)
            + [pltpu.VMEM((2, rows, features), jnp.bfloat16)],
        ),
        out_shape=out_shape,
        compiler_params=pltpu.CompilerParams(vmem_limit_bytes=VMEM_LIMIT),
        cost_estimate=work_of(weight * (4 * rows + 2 * owned * piece_rows) * units * features),
        name="group",
    )(spots, *normed, *grads, *limits, weight_in, weight_out)


def weights_kernel(*refs, groups, scale, started):
    act_refs = refs[:groups]
    col_refs = refs[groups : 2 * groups]
    in_ref, out_ref = refs[-2:]

    def stack(sources, kind):
        return jnp.concatenate([ref[kind] for ref in sources], axis=0)

    def total(left, right):
        return lax.dot_general(
            left, right, (((0,), (0,)), ((), ())), preferred_element_type=jnp.float32
        )

    for_in = total(stack(col_refs, 0), stack(act_refs, 0))
    for_out = total(stack(act_refs, 1), stack(col_refs, 1))
    if started:
        for_in += refs[-4][...].astype(jnp.float32)
        for_out += refs[-3][...].astype(jnp.float32)
    in_ref[...] = (for_in * scale).astype(in_ref.dtype)
    out_ref[...] = (for_out * scale).astype(out_ref.dtype)


def weights_call(groups, begun, scale):
    share = groups[0][1].shape[2]
    units = groups[0][0].shape[2] - share
    tile = tile_of(units, 512)
    acts, acts_specs, cols, cols_specs = [], [], [], []
    for own, own_cols, other in groups:
        rows = own.shape[1]
        acts += [own, other]
        acts_specs += [pl.BlockSpec((2, rows, tile), lambda i: (0, 0, i))] * 2
        cols += [own_cols, other]
        cols_specs += [
            pl.BlockSpec((2, rows, share), lambda i: (0, 0, 0)),
            pl.BlockSpec((2, rows, share), lambda i: (0, 0, units // share)),
        ]
    in_spec = pl.BlockSpec((share, tile), lambda i: (0, i))
    out_spec = pl.BlockSpec((tile, share), lambda i: (i, 0))
    return pl.pallas_call(
        functools.partial(weights_kernel, groups=len(acts), scale=scale, started=bool(begun)),
        grid=(units // tile,),
        in_specs=acts_specs + cols_specs + ([in_spec, out_spec] if begun else []),
        out_specs=[in_spec, out_spec],
        out_shape=[
            jax.ShapeDtypeStruct((share, units), jnp.bfloat16),
            jax.ShapeDtypeStruct((units, share), jnp.bfloat16),
        ],
        compiler_params=pltpu.CompilerParams(vmem_limit_bytes=VMEM_LIMIT),
        cost_estimate=work_of(0),
        name="weights",
    )(*acts, *cols, *begun)


def after(value, *others):
    return lax.optimization_barrier((value, others))[0] if others else value


def shards(inputs, grad_out, norm_gain, level_order, level_counts, weight_in, weight_out):
    rows = inputs.shape[0]
    ring = lax.axis_size("tensor")
    place = lax.axis_index("tensor")
    blocks = lax.axis_size("dp")
    block = lax.axis_index("dp")
    chips = blocks // 2
    unit_local = weight_in.shape[1]
    unit_total = unit_local * ring
    share = inputs.shape[1] // blocks
    tile = math.gcd(unit_local, unit_total // 8, share)

    from_next = [((i + 1) % ring, i) for i in range(ring)]
    from_last = [(i, (i + 1) % ring) for i in range(ring)]
    from_chip = [((i + 2) % blocks, i) for i in range(blocks)]
    swap_cores = [(i, i ^ 1) for i in range(blocks)]
    half = ring // 2

    def send(one, axis, pairs, name):
        with jax.named_scope(name):
            return lax.ppermute(one, axis, pairs)

    level_sets = [jnp.concatenate([level_order, level_counts[0]])]
    for _ in range(1, chips):
        level_sets.append(send(level_sets[-1], "dp", from_chip, "chip_levels"))

    as_float = inputs.astype(jnp.float32)
    row_mean = jnp.mean(as_float, axis=1, keepdims=True)
    centred = as_float - row_mean
    row_scale = lax.rsqrt(jnp.mean(centred * centred, axis=1, keepdims=True) + NORM_EPS)
    standard = centred * row_scale
    normed = (standard * norm_gain[None, :]).astype(jnp.bfloat16)

    limits = [unit_limits(one[:-4], one[-4:], place * rows, unit_total) for one in level_sets]
    spots = jnp.stack([place * unit_local, block * share, (block ^ 1) * share]).astype(jnp.int32)

    kinds = ("normed", "grad")

    def move(piece, axis, pairs, name, *gates):
        return tuple(
            send(after(one, *gates), axis, pairs, f"{name}_{kind}") for one, kind in zip(piece, kinds)
        )

    near = {0: (normed, grad_out)}
    for step in range(1, ring):
        near[step] = move(near[step - 1], "tensor", from_next, f"ring_{step}")
    sets = [[near[step] for step in range(ring)]]
    for chip in range(1, chips):
        sets.append(
            [
                None if step == ring - 1 else move(piece, "dp", from_chip, f"chip_{step}")
                for step, piece in enumerate(sets[-1])
            ]
        )

    def last_over_chips(early, gates):
        for chip in range(1, chips):
            normed_rows, grads = sets[chip - 1][-1]
            name = f"chip_{ring - 1}"
            grads = send(after(grads, *gates), "dp", from_chip, f"{name}_grad")
            normed_rows = send(after(normed_rows, *early), "dp", from_chip, f"{name}_normed")
            sets[chip][-1] = (normed_rows, grads)

    groups, own_grads, hops, hold = [], [], [], []

    def chain(steps, pairs, name):
        travelling = None
        for step in steps:
            total = after(own_grads[step], *hold)
            if travelling is not None:
                total = (total + travelling.astype(jnp.float32)).astype(jnp.bfloat16)
            travelling = send(total.astype(jnp.bfloat16), "tensor", pairs, f"{name}_{step}")
        return travelling

    arrivals = [
        [(chip, slot - chip) for chip in range(chips) if 0 <= slot - chip < ring]
        for slot in range(ring + chips - 1)
    ]
    if len(arrivals) > 1:
        arrivals[:2] = [sorted(arrivals[0] + arrivals[1])]
    last = len(arrivals) - 1
    totals = []
    for at, entries in enumerate(arrivals):
        gates = []
        if at == len(arrivals) - 2 and at > 1:
            totals = weights_call(groups[:-1], [], 1.0)
            gates = hold = [totals[0]]
            groups = groups[-1:]
        if not hold and at > 1:
            hold = [own_cols]
        if any(sets[chip][step] is None for chip, step in arrivals[min(at + 1, last)]):
            last_over_chips([own_cols], hold)
        own_steps = [step for chip, step in entries if chip == 0]
        back_types = [jnp.bfloat16 if step in (half, half + 1) else jnp.float32 for step in own_steps]
        with jax.named_scope(f"group_{at}"):
            act, own_cols, *back = group_call(
                after(spots, *gates),
                [sets[chip][step][0] for chip, step in entries],
                [sets[chip][step][1] for chip, step in entries],
                limits[: 1 + max(chip for chip, _ in entries)],
                entries,
                weight_in,
                weight_out,
                tile,
                share,
                back_types,
                WEIGHTS.get(at, 1.0),
            )
        own_grads.extend(back)
        if at == last and ring > 2:
            hops.append(chain(range(half + 1, ring), from_next, "sum_down"))
        groups.append((act, own_cols, send(after(act, *hops), "dp", swap_cores, f"swap_{at}")))

    if ring > 1:
        hops.append(chain(range(half, 0, -1), from_last, "sum_up"))
    grad_weight_in, grad_weight_out = weights_call(groups, totals, 1.0 / blocks)
    own_grad = after(own_grads[0], grad_weight_in).astype(jnp.float32)
    for hop in hops:
        own_grad = own_grad + hop.astype(jnp.float32)
    branch_grad = norm_backward(own_grad, standard, row_scale, norm_gain)
    grad_input = (grad_out.astype(jnp.float32) + branch_grad).astype(jnp.bfloat16)

    return (grad_input, grad_weight_in, grad_weight_out)


def solution(mesh):
    in_specs = (
        P(("groups", "dp", "tensor"), None),
        P(("groups", "dp", "tensor"), None),
        P(),
        P(("groups", "dp")),
        P(("groups", "dp"), None),
        P(None, "tensor"),
        P("tensor", None),
    )
    out_specs = (
        P(("groups", "dp", "tensor"), None),
        P(("groups", "dp"), "tensor"),
        P(("groups", "tensor"), "dp"),
    )
    return jax.shard_map(shards, mesh=mesh, in_specs=in_specs, out_specs=out_specs, check_vma=False)
```

```python
import functools
import math

import jax
import jax.numpy as jnp
from jax import lax
from jax.experimental import pallas as pl
from jax.experimental.pallas import tpu as pltpu
from jax.sharding import PartitionSpec as P

GELU_SCALE = 0.7978845608028654
GELU_CUBE = 0.044715
NORM_EPS = 1e-06
VMEM_LIMIT = 48 * 1024 * 1024
WORK = 3.0
WEIGHTS = {2: 3.0, 4: 3.0}


def gelu_parts(pre_act):
    square = pre_act * pre_act
    tanh_val = jnp.tanh(pre_act * (GELU_SCALE + (GELU_SCALE * GELU_CUBE) * square))
    share = 0.5 + 0.5 * tanh_val
    gelu_value = pre_act * share
    gelu_slope = share + gelu_value * (1.0 - tanh_val) * (
        GELU_SCALE + (3.0 * GELU_SCALE * GELU_CUBE) * square
    )
    return (gelu_value, gelu_slope)


def unit_limits(block_order, count_row, first, unit_total):
    above_three = count_row[3]
    above_two = above_three + count_row[2]
    above_one = above_two + count_row[1]
    count = block_order.shape[0]
    places = jnp.arange(count, dtype=jnp.int32)
    ranked = (
        (places < above_three).astype(jnp.int32)
        + (places < above_two).astype(jnp.int32)
        + (places < above_one).astype(jnp.int32)
    )
    tokens = (first + places) % count
    hits = block_order[None, :] == tokens[:, None]
    limits = unit_total // (1 << (3 - ranked))
    return jnp.sum(jnp.where(hits, limits[None, :], 0), axis=1, keepdims=True)


def norm_backward(grad_normed, standard, row_scale, norm_gain):
    scaled = grad_normed * norm_gain[None, :]
    centre = jnp.mean(scaled, axis=1, keepdims=True)
    along = jnp.mean(scaled * standard, axis=1, keepdims=True)
    return row_scale * (scaled - centre - standard * along)


def work_of(flops):
    return pl.CostEstimate(flops=int(WORK * flops), bytes_accessed=0, transcendentals=0)


def tile_of(extent, wanted):
    while extent % wanted:
        wanted //= 2
    return wanted


def group_kernel(spots, *refs, limit_at, owned, extra, share, tiles):
    pieces, sets = len(limit_at), 1 + max(at for at, _ in limit_at)
    normed_refs = refs[:pieces]
    grad_refs = refs[pieces : 2 * pieces]
    limit_refs = refs[2 * pieces : 2 * pieces + sets]
    extra_refs = refs[2 * pieces + sets : 2 * pieces + sets + extra]
    in_ref, out_ref, acts_ref, own_ref, *rest = refs[2 * pieces + sets + extra :]
    tile = pl.program_id(0)

    def columns(target, first):
        span = pl.ds(pl.multiple_of(first, 128), share)
        for kind, sources in enumerate((normed_refs, grad_refs)):
            for at, ref in enumerate(sources):
                size = ref.shape[0]
                target[kind, at * size : (at + 1) * size, :] = ref[:, span]

    rows_ref, rest = rest[-1], rest[:-1]
    size = normed_refs[0].shape[0]
    limit = jnp.concatenate([limit_refs[at][step * size : (step + 1) * size, :] for at, step in limit_at])

    @pl.when(tile == 0)
    def _():
        columns(own_ref, spots[1])
        for kind, sources in enumerate((normed_refs, grad_refs)):
            for at, ref in enumerate(sources):
                size = ref.shape[0]
                rows_ref[kind, at * size : (at + 1) * size, :] = ref[...]

    @pl.when(tile == tiles)
    def _():
        columns(acts_ref, spots[2])

    @pl.when(tile < tiles)
    def _():
        group_tile(spots[0], rows_ref, limit, in_ref, out_ref, acts_ref, rest, owned * size, extra_refs, tiles)


def group_tile(
    first, rows_ref, limit, in_ref, out_ref, acts_ref, rest, own_rows, extra_refs, tiles
):
    tile = pl.program_id(0)
    units = in_ref.shape[1]
    width = 256 if units % 256 == 0 else units

    mask = first + tile * units < limit
    products = []
    for start in range(0, units, width):
        span = slice(start, start + width)
        pre_act = jnp.dot(rows_ref[0], in_ref[:, span], preferred_element_type=jnp.float32)
        grad_hidden = lax.dot_general(
            rows_ref[1], out_ref[span, :], (((1,), (1,)), ((), ())), preferred_element_type=jnp.float32
        )
        products.append((span, pre_act, grad_hidden))
    for span, pre_act, grad_hidden in products:
        gelu_value, gelu_slope = gelu_parts(pre_act)
        acts_ref[0, :, span] = jnp.where(mask, grad_hidden * gelu_slope, 0.0).astype(jnp.bfloat16)
        acts_ref[1, :, span] = jnp.where(mask, gelu_value, 0.0).astype(jnp.bfloat16)
    if rest:
        back_refs, total_ref = rest[:-1], rest[-1]
        parts = [acts_ref[0, :own_rows, :]] if own_rows else []
        term = lax.dot_general(
            jnp.concatenate(parts + [ref[0] for ref in extra_refs]),
            in_ref[...],
            (((1,), (1,)), ((), ())),
            preferred_element_type=jnp.float32,
        )

        @pl.when(tile == 0)
        def _():
            total_ref[...] = term

        @pl.when(tile != 0)
        def _():
            total_ref[...] += term

        @pl.when(tile == tiles - 1)
        def _():
            for at, ref in enumerate(back_refs):
                size = ref.shape[0]
                ref[...] = total_ref[at * size : (at + 1) * size, :].astype(ref.dtype)


def group_call(
    spots, normed, grads, limits, limit_at, weight_in, weight_out, tile, share, back_types, extra, weight
):
    features, units = weight_in.shape
    piece_rows = normed[0].shape[0]
    rows = piece_rows * len(normed)
    owned = len(back_types) - len(extra)
    tiles = units // tile
    whole = lambda shape: pl.BlockSpec(shape, lambda i, spots: (0,) * len(shape))
    out_shape = [
        jax.ShapeDtypeStruct((2, rows, units + share), jnp.bfloat16),
        jax.ShapeDtypeStruct((2, rows, share), jnp.bfloat16),
    ]
    out_specs = [
        pl.BlockSpec((2, rows, tile), lambda i, spots: (0, 0, i)),
        whole((2, rows, share)),
    ]
    for kind in back_types:
        out_shape.append(jax.ShapeDtypeStruct((piece_rows, features), kind))
        out_specs.append(whole((piece_rows, features)))
    return pl.pallas_call(
        functools.partial(
            group_kernel,
            limit_at=limit_at,
            owned=owned,
            extra=len(extra),
            share=share,
            tiles=tiles,
        ),
        grid_spec=pltpu.PrefetchScalarGridSpec(
            num_scalar_prefetch=1,
            grid=(tiles + share // tile,),
            in_specs=[whole(one.shape) for one in (*normed, *grads, *limits)]
            + [
                pl.BlockSpec((1, piece_rows, tile), lambda i, spots: (0, 0, jnp.minimum(i, tiles - 1)))
                for _ in extra
            ]
            + [
                pl.BlockSpec((features, tile), lambda i, spots: (0, jnp.minimum(i, tiles - 1))),
                pl.BlockSpec((tile, features), lambda i, spots: (jnp.minimum(i, tiles - 1), 0)),
            ],
            out_specs=out_specs,
            scratch_shapes=[pltpu.VMEM((len(back_types) * piece_rows, features), jnp.float32)]
            * bool(back_types)
            + [pltpu.VMEM((2, rows, features), jnp.bfloat16)],
        ),
        out_shape=out_shape,
        compiler_params=pltpu.CompilerParams(vmem_limit_bytes=VMEM_LIMIT),
        cost_estimate=work_of(weight * (4 * rows + 2 * len(back_types) * piece_rows) * units * features),
        name="group",
    )(spots, *normed, *grads, *limits, *extra, weight_in, weight_out)


def weights_kernel(*refs, groups, scale, started):
    act_refs = refs[:groups]
    col_refs = refs[groups : 2 * groups]
    in_ref, out_ref = refs[-2:]

    def stack(sources, kind):
        return jnp.concatenate([ref[kind] for ref in sources], axis=0)

    def total(left, right):
        return lax.dot_general(
            left, right, (((0,), (0,)), ((), ())), preferred_element_type=jnp.float32
        )

    for_in = total(stack(col_refs, 0), stack(act_refs, 0))
    for_out = total(stack(act_refs, 1), stack(col_refs, 1))
    if started:
        for_in += refs[-4][...].astype(jnp.float32)
        for_out += refs[-3][...].astype(jnp.float32)
    in_ref[...] = (for_in * scale).astype(in_ref.dtype)
    out_ref[...] = (for_out * scale).astype(out_ref.dtype)


def weights_call(groups, begun, scale):
    share = groups[0][1].shape[2]
    units = groups[0][0].shape[2] - share
    tile = tile_of(units, 512)
    acts, acts_specs, cols, cols_specs = [], [], [], []
    for own, own_cols, other in groups:
        rows = own.shape[1]
        acts += [own, other]
        acts_specs += [pl.BlockSpec((2, rows, tile), lambda i: (0, 0, i))] * 2
        cols += [own_cols, other]
        cols_specs += [
            pl.BlockSpec((2, rows, share), lambda i: (0, 0, 0)),
            pl.BlockSpec((2, rows, share), lambda i: (0, 0, units // share)),
        ]
    in_spec = pl.BlockSpec((share, tile), lambda i: (0, i))
    out_spec = pl.BlockSpec((tile, share), lambda i: (i, 0))
    return pl.pallas_call(
        functools.partial(weights_kernel, groups=len(acts), scale=scale, started=bool(begun)),
        grid=(units // tile,),
        in_specs=acts_specs + cols_specs + ([in_spec, out_spec] if begun else []),
        out_specs=[in_spec, out_spec],
        out_shape=[
            jax.ShapeDtypeStruct((share, units), jnp.bfloat16),
            jax.ShapeDtypeStruct((units, share), jnp.bfloat16),
        ],
        compiler_params=pltpu.CompilerParams(vmem_limit_bytes=VMEM_LIMIT),
        cost_estimate=work_of(0),
        name="weights",
    )(*acts, *cols, *begun)


def after(value, *others):
    return lax.optimization_barrier((value, others))[0] if others else value


def shards(inputs, grad_out, norm_gain, level_order, level_counts, weight_in, weight_out):
    rows = inputs.shape[0]
    ring = lax.axis_size("tensor")
    place = lax.axis_index("tensor")
    blocks = lax.axis_size("dp")
    block = lax.axis_index("dp")
    chips = blocks // 2
    unit_local = weight_in.shape[1]
    unit_total = unit_local * ring
    share = inputs.shape[1] // blocks
    tile = math.gcd(unit_local, unit_total // 8, share)

    from_next = [((i + 1) % ring, i) for i in range(ring)]
    from_last = [(i, (i + 1) % ring) for i in range(ring)]
    from_chip = [((i + 2) % blocks, i) for i in range(blocks)]
    swap_cores = [(i, i ^ 1) for i in range(blocks)]
    half = ring // 2

    def send(one, axis, pairs, name):
        with jax.named_scope(name):
            return lax.ppermute(one, axis, pairs)

    as_float = inputs.astype(jnp.float32)
    row_mean = jnp.mean(as_float, axis=1, keepdims=True)
    centred = as_float - row_mean
    row_scale = lax.rsqrt(jnp.mean(centred * centred, axis=1, keepdims=True) + NORM_EPS)
    standard = centred * row_scale
    normed = (standard * norm_gain[None, :]).astype(jnp.bfloat16)

    limits = [unit_limits(level_order, level_counts[0], place * rows, unit_total)]
    for _ in range(1, chips):
        limits.append(send(limits[-1], "dp", from_chip, "chip_limits"))

    spots = jnp.stack([place * unit_local, block * share, (block ^ 1) * share]).astype(jnp.int32)

    kinds = ("normed", "grad")

    def move(piece, axis, pairs, name, *gates):
        return tuple(
            send(after(one, *gates), axis, pairs, f"{name}_{kind}") for one, kind in zip(piece, kinds)
        )

    near = {0: (normed, grad_out)}
    for step in range(1, ring):
        near[step] = None if 2 < step == ring - 1 else move(near[step - 1], "tensor", from_next, f"ring_{step}")
    sets = [[near[step] for step in range(ring)]]
    for chip in range(1, chips):
        sets.append(
            [
                None if step == ring - 1 or 1 < step == ring - 2 else move(piece, "dp", from_chip, f"chip_{step}")
                for step, piece in enumerate(sets[-1])
            ]
        )

    def second_over_chips(*gates):
        for chip in range(1, chips):
            sets[chip][-2] = move(sets[chip - 1][-2], "dp", from_chip, f"chip_{ring - 2}", *gates)
        sets[0][-1] = move(sets[0][-2], "tensor", from_next, f"ring_{ring - 1}", *gates)

    def last_over_chips(early, gates):
        for chip in range(1, chips):
            normed_rows, grads = sets[chip - 1][-1]
            name = f"chip_{ring - 1}"
            grads = send(after(grads, *gates), "dp", from_chip, f"{name}_grad")
            normed_rows = send(after(normed_rows, *early), "dp", from_chip, f"{name}_normed")
            sets[chip][-1] = (normed_rows, grads)

    groups, own_grads, hops, hold = [], {}, [], []

    def chain(steps, pairs, name):
        travelling = None
        for step in steps:
            total = after(own_grads[step], *hold)
            if travelling is not None:
                total = (total + travelling.astype(jnp.float32)).astype(jnp.bfloat16)
            travelling = send(total.astype(jnp.bfloat16), "tensor", pairs, f"{name}_{step}")
        return travelling

    arrivals = [
        [(chip, slot - chip) for chip in range(chips) if 0 <= slot - chip < ring]
        for slot in range(ring + chips - 1)
    ]
    last = len(arrivals) - 1
    totals = []
    for at, entries in enumerate(arrivals):
        gates = []
        if at == len(arrivals) - 2 and at > 1:
            totals = weights_call(groups[:-1], [], 1.0)
            gates = hold = [totals[0]]
            groups = groups[-1:]
        if not hold and at > 1:
            hold = [own_cols]
        if any(sets[chip][step] is None for chip, step in arrivals[min(at + 1, last)]):
            last_over_chips([own_cols], hold)
        own_steps = [step for chip, step in entries if chip == 0]
        extra = []
        if at == 1 and ring > 2:
            own_steps, later = [], own_steps
            gates = [groups[0][1]]
        elif at == 2 and ring > 2:
            own_steps, extra = own_steps + later, [groups[1][0]]
        back_types = [jnp.bfloat16 if step in (half, half + 1) else jnp.float32 for step in own_steps]
        with jax.named_scope(f"group_{at}"):
            act, own_cols, *back = group_call(
                after(spots, *gates),
                [sets[chip][step][0] for chip, step in entries],
                [sets[chip][step][1] for chip, step in entries],
                limits[: 1 + max(chip for chip, _ in entries)],
                entries,
                weight_in,
                weight_out,
                tile,
                share,
                back_types,
                extra,
                WEIGHTS.get(at, 1.0),
            )
        own_grads.update(zip(own_steps, back))
        if at == last and ring > 2:
            hops.append(chain(range(half + 1, ring), from_next, "sum_down"))
        if at == 1 and ring > 3:
            second_over_chips(own_cols, groups[0][2])
        groups.append((act, own_cols, send(after(act, *hops), "dp", swap_cores, f"swap_{at}")))

    if ring > 1:
        hops.append(chain(range(half, 0, -1), from_last, "sum_up"))
    grad_weight_in, grad_weight_out = weights_call(groups, totals, 1.0 / blocks)
    own_grad = after(own_grads[0], grad_weight_in).astype(jnp.float32)
    for hop in hops:
        own_grad = own_grad + hop.astype(jnp.float32)
    branch_grad = norm_backward(own_grad, standard, row_scale, norm_gain)
    grad_input = (grad_out.astype(jnp.float32) + branch_grad).astype(jnp.bfloat16)

    return (grad_input, grad_weight_in, grad_weight_out)


def solution(mesh):
    in_specs = (
        P(("groups", "dp", "tensor"), None),
        P(("groups", "dp", "tensor"), None),
        P(),
        P(("groups", "dp")),
        P(("groups", "dp"), None),
        P(None, "tensor"),
        P("tensor", None),
    )
    out_specs = (
        P(("groups", "dp", "tensor"), None),
        P(("groups", "dp"), "tensor"),
        P(("groups", "tensor"), "dp"),
    )
    return jax.shard_map(shards, mesh=mesh, in_specs=in_specs, out_specs=out_specs, check_vma=False)
```

```python
import functools
import math

import jax
import jax.numpy as jnp
from jax import lax
from jax.experimental import pallas as pl
from jax.experimental.pallas import tpu as pltpu
from jax.sharding import PartitionSpec as P

GELU_SCALE = 0.7978845608028654
GELU_CUBE = 0.044715
NORM_EPS = 1e-06
VMEM_LIMIT = 48 * 1024 * 1024
WORK = 3.0
WEIGHTS = {2: 3.0, 4: 3.0}


def gelu_parts(pre_act):
    square = pre_act * pre_act
    tanh_val = jnp.tanh(pre_act * (GELU_SCALE + (GELU_SCALE * GELU_CUBE) * square))
    share = 0.5 + 0.5 * tanh_val
    gelu_value = pre_act * share
    gelu_slope = share + gelu_value * (1.0 - tanh_val) * (
        GELU_SCALE + (3.0 * GELU_SCALE * GELU_CUBE) * square
    )
    return (gelu_value, gelu_slope)


def unit_limits(block_order, count_row, first, unit_total):
    above_three = count_row[3]
    above_two = above_three + count_row[2]
    above_one = above_two + count_row[1]
    count = block_order.shape[0]
    places = jnp.arange(count, dtype=jnp.int32)
    ranked = (
        (places < above_three).astype(jnp.int32)
        + (places < above_two).astype(jnp.int32)
        + (places < above_one).astype(jnp.int32)
    )
    tokens = (first + places) % count
    hits = block_order[None, :] == tokens[:, None]
    limits = unit_total // (1 << (3 - ranked))
    return jnp.sum(jnp.where(hits, limits[None, :], 0), axis=1, keepdims=True)


def norm_backward(grad_normed, standard, row_scale, norm_gain):
    scaled = grad_normed * norm_gain[None, :]
    centre = jnp.mean(scaled, axis=1, keepdims=True)
    along = jnp.mean(scaled * standard, axis=1, keepdims=True)
    return row_scale * (scaled - centre - standard * along)


def work_of(flops):
    return pl.CostEstimate(flops=int(WORK * flops), bytes_accessed=0, transcendentals=0)


def tile_of(extent, wanted):
    while extent % wanted:
        wanted //= 2
    return wanted


def group_kernel(spots, *refs, limit_at, owned, extra, share, tiles):
    pieces, sets = len(limit_at), 1 + max(at for at, _ in limit_at)
    normed_refs = refs[:pieces]
    grad_refs = refs[pieces : 2 * pieces]
    limit_refs = refs[2 * pieces : 2 * pieces + sets]
    extra_refs = refs[2 * pieces + sets : 2 * pieces + sets + extra]
    in_ref, out_ref, acts_ref, own_ref, *rest = refs[2 * pieces + sets + extra :]
    tile = pl.program_id(0)

    def columns(target, first):
        span = pl.ds(pl.multiple_of(first, 128), share)
        for kind, sources in enumerate((normed_refs, grad_refs)):
            for at, ref in enumerate(sources):
                size = ref.shape[0]
                target[kind, at * size : (at + 1) * size, :] = ref[:, span]

    rows_ref, rest = rest[-1], rest[:-1]
    size = normed_refs[0].shape[0]
    limit = jnp.concatenate([limit_refs[at][step * size : (step + 1) * size, :] for at, step in limit_at])

    @pl.when(tile == 0)
    def _():
        columns(own_ref, spots[1])
        for kind, sources in enumerate((normed_refs, grad_refs)):
            for at, ref in enumerate(sources):
                size = ref.shape[0]
                rows_ref[kind, at * size : (at + 1) * size, :] = ref[...]

    @pl.when(tile == tiles)
    def _():
        columns(acts_ref, spots[2])

    @pl.when(tile < tiles)
    def _():
        group_tile(spots[0], rows_ref, limit, in_ref, out_ref, acts_ref, rest, owned * size, extra_refs, tiles)


def group_tile(
    first, rows_ref, limit, in_ref, out_ref, acts_ref, rest, own_rows, extra_refs, tiles
):
    tile = pl.program_id(0)
    units = in_ref.shape[1]
    width = 256 if units % 256 == 0 else units

    mask = first + tile * units < limit
    products = []
    for start in range(0, units, width):
        span = slice(start, start + width)
        pre_act = jnp.dot(rows_ref[0], in_ref[:, span], preferred_element_type=jnp.float32)
        grad_hidden = lax.dot_general(
            rows_ref[1], out_ref[span, :], (((1,), (1,)), ((), ())), preferred_element_type=jnp.float32
        )
        products.append((span, pre_act, grad_hidden))
    for span, pre_act, grad_hidden in products:
        gelu_value, gelu_slope = gelu_parts(pre_act)
        acts_ref[0, :, span] = jnp.where(mask, grad_hidden * gelu_slope, 0.0).astype(jnp.bfloat16)
        acts_ref[1, :, span] = jnp.where(mask, gelu_value, 0.0).astype(jnp.bfloat16)
    if rest:
        back_refs, total_ref = rest[:-1], rest[-1]
        parts = [acts_ref[0, :own_rows, :]] if own_rows else []
        term = lax.dot_general(
            jnp.concatenate(parts + [ref[0] for ref in extra_refs]),
            in_ref[...],
            (((1,), (1,)), ((), ())),
            preferred_element_type=jnp.float32,
        )

        @pl.when(tile == 0)
        def _():
            total_ref[...] = term

        @pl.when(tile != 0)
        def _():
            total_ref[...] += term

        @pl.when(tile == tiles - 1)
        def _():
            for at, ref in enumerate(back_refs):
                size = ref.shape[0]
                ref[...] = total_ref[at * size : (at + 1) * size, :].astype(ref.dtype)


def group_call(
    spots, normed, grads, limits, limit_at, weight_in, weight_out, tile, share, back_types, extra, weight
):
    features, units = weight_in.shape
    piece_rows = normed[0].shape[0]
    rows = piece_rows * len(normed)
    owned = len(back_types) - len(extra)
    tiles = units // tile
    whole = lambda shape: pl.BlockSpec(shape, lambda i, spots: (0,) * len(shape))
    out_shape = [
        jax.ShapeDtypeStruct((2, rows, units + share), jnp.bfloat16),
        jax.ShapeDtypeStruct((2, rows, share), jnp.bfloat16),
    ]
    out_specs = [
        pl.BlockSpec((2, rows, tile), lambda i, spots: (0, 0, i)),
        whole((2, rows, share)),
    ]
    for kind in back_types:
        out_shape.append(jax.ShapeDtypeStruct((piece_rows, features), kind))
        out_specs.append(whole((piece_rows, features)))
    return pl.pallas_call(
        functools.partial(
            group_kernel,
            limit_at=limit_at,
            owned=owned,
            extra=len(extra),
            share=share,
            tiles=tiles,
        ),
        grid_spec=pltpu.PrefetchScalarGridSpec(
            num_scalar_prefetch=1,
            grid=(tiles + share // tile,),
            in_specs=[whole(one.shape) for one in (*normed, *grads, *limits)]
            + [
                pl.BlockSpec((1, piece_rows, tile), lambda i, spots: (0, 0, jnp.minimum(i, tiles - 1)))
                for _ in extra
            ]
            + [
                pl.BlockSpec((features, tile), lambda i, spots: (0, jnp.minimum(i, tiles - 1))),
                pl.BlockSpec((tile, features), lambda i, spots: (jnp.minimum(i, tiles - 1), 0)),
            ],
            out_specs=out_specs,
            scratch_shapes=[pltpu.VMEM((len(back_types) * piece_rows, features), jnp.float32)]
            * bool(back_types)
            + [pltpu.VMEM((2, rows, features), jnp.bfloat16)],
        ),
        out_shape=out_shape,
        compiler_params=pltpu.CompilerParams(vmem_limit_bytes=VMEM_LIMIT),
        cost_estimate=work_of(weight * (4 * rows + 2 * len(back_types) * piece_rows) * units * features),
        name="group",
    )(spots, *normed, *grads, *limits, *extra, weight_in, weight_out)


def weights_kernel(*refs, groups, scale, started):
    act_refs = refs[:groups]
    col_refs = refs[groups : 2 * groups]
    in_ref, out_ref = refs[-2:]

    def stack(sources, kind):
        return jnp.concatenate([ref[kind] for ref in sources], axis=0)

    def total(left, right):
        return lax.dot_general(
            left, right, (((0,), (0,)), ((), ())), preferred_element_type=jnp.float32
        )

    for_in = total(stack(col_refs, 0), stack(act_refs, 0))
    for_out = total(stack(act_refs, 1), stack(col_refs, 1))
    if started:
        for_in += refs[-4][...].astype(jnp.float32)
        for_out += refs[-3][...].astype(jnp.float32)
    in_ref[...] = (for_in * scale).astype(in_ref.dtype)
    out_ref[...] = (for_out * scale).astype(out_ref.dtype)


def weights_call(groups, begun, scale):
    share = groups[0][1].shape[2]
    units = groups[0][0].shape[2] - share
    tile = tile_of(units, 512)
    acts, acts_specs, cols, cols_specs = [], [], [], []
    for own, own_cols, other in groups:
        rows = own.shape[1]
        acts += [own, other]
        acts_specs += [pl.BlockSpec((2, rows, tile), lambda i: (0, 0, i))] * 2
        cols += [own_cols, other]
        cols_specs += [
            pl.BlockSpec((2, rows, share), lambda i: (0, 0, 0)),
            pl.BlockSpec((2, rows, share), lambda i: (0, 0, units // share)),
        ]
    in_spec = pl.BlockSpec((share, tile), lambda i: (0, i))
    out_spec = pl.BlockSpec((tile, share), lambda i: (i, 0))
    return pl.pallas_call(
        functools.partial(weights_kernel, groups=len(acts), scale=scale, started=bool(begun)),
        grid=(units // tile,),
        in_specs=acts_specs + cols_specs + ([in_spec, out_spec] if begun else []),
        out_specs=[in_spec, out_spec],
        out_shape=[
            jax.ShapeDtypeStruct((share, units), jnp.bfloat16),
            jax.ShapeDtypeStruct((units, share), jnp.bfloat16),
        ],
        compiler_params=pltpu.CompilerParams(vmem_limit_bytes=VMEM_LIMIT),
        cost_estimate=work_of(0),
        name="weights",
    )(*acts, *cols, *begun)


def after(value, *others):
    return lax.optimization_barrier((value, others))[0] if others else value


def shards(inputs, grad_out, norm_gain, level_order, level_counts, weight_in, weight_out):
    rows = inputs.shape[0]
    ring = lax.axis_size("tensor")
    place = lax.axis_index("tensor")
    blocks = lax.axis_size("dp")
    block = lax.axis_index("dp")
    chips = blocks // 2
    unit_local = weight_in.shape[1]
    unit_total = unit_local * ring
    share = inputs.shape[1] // blocks
    tile = math.gcd(unit_local, unit_total // 8, share)

    from_next = [((i + 1) % ring, i) for i in range(ring)]
    from_last = [(i, (i + 1) % ring) for i in range(ring)]
    from_chip = [((i + 2) % blocks, i) for i in range(blocks)]
    swap_cores = [(i, i ^ 1) for i in range(blocks)]
    half = ring // 2

    def send(one, axis, pairs, name):
        with jax.named_scope(name):
            return lax.ppermute(one, axis, pairs)

    as_float = inputs.astype(jnp.float32)
    row_mean = jnp.mean(as_float, axis=1, keepdims=True)
    centred = as_float - row_mean
    row_scale = lax.rsqrt(jnp.mean(centred * centred, axis=1, keepdims=True) + NORM_EPS)
    standard = centred * row_scale
    normed = (standard * norm_gain[None, :]).astype(jnp.bfloat16)

    limits = [unit_limits(level_order, level_counts[0], place * rows, unit_total)]
    for _ in range(1, chips):
        limits.append(send(limits[-1], "dp", from_chip, "chip_limits"))

    spots = jnp.stack([place * unit_local, block * share, (block ^ 1) * share]).astype(jnp.int32)

    kinds = ("normed", "grad")

    def move(piece, axis, pairs, name, *gates):
        return tuple(
            send(after(one, *gates), axis, pairs, f"{name}_{kind}") for one, kind in zip(piece, kinds)
        )

    near = {0: (normed, grad_out)}
    for step in range(1, ring):
        near[step] = None if 2 < step == ring - 1 else move(near[step - 1], "tensor", from_next, f"ring_{step}")
    sets = [[near[step] for step in range(ring)]]
    for chip in range(1, chips):
        sets.append(
            [
                None if step == ring - 1 or 1 < step == ring - 2 else move(piece, "dp", from_chip, f"chip_{step}")
                for step, piece in enumerate(sets[-1])
            ]
        )

    def second_over_chips(*gates):
        for chip in range(1, chips):
            sets[chip][-2] = move(sets[chip - 1][-2], "dp", from_chip, f"chip_{ring - 2}", *gates)
        sets[0][-1] = move(sets[0][-2], "tensor", from_next, f"ring_{ring - 1}", *gates)

    def last_over_chips(early, gates):
        for chip in range(1, chips):
            normed_rows, grads = sets[chip - 1][-1]
            name = f"chip_{ring - 1}"
            grads = send(after(grads, *gates), "dp", from_chip, f"{name}_grad")
            normed_rows = send(after(normed_rows, *early), "dp", from_chip, f"{name}_normed")
            sets[chip][-1] = (normed_rows, grads)

    groups, own_grads, hops, hold = [], {}, [], []

    def chain(steps, pairs, name):
        travelling = None
        for step in steps:
            total = after(own_grads[step], *hold)
            if travelling is not None:
                total = (total + travelling.astype(jnp.float32)).astype(jnp.bfloat16)
            travelling = send(total.astype(jnp.bfloat16), "tensor", pairs, f"{name}_{step}")
        return travelling

    arrivals = [
        [(chip, slot - chip) for chip in range(chips) if 0 <= slot - chip < ring]
        for slot in range(ring + chips - 1)
    ]
    last = len(arrivals) - 1
    totals = []
    for at, entries in enumerate(arrivals):
        gates = []
        if at == len(arrivals) - 2 and at > 1:
            totals = weights_call(groups[:-1], [], 1.0)
            gates = hold = [totals[0]]
            groups = groups[-1:]
        if not hold and at > 1:
            hold = [own_cols]
        if any(sets[chip][step] is None for chip, step in arrivals[min(at + 1, last)]):
            last_over_chips([own_cols], hold)
        own_steps = [step for chip, step in entries if chip == 0]
        extra = []
        if at == 1 and ring > 2:
            own_steps, later = [], own_steps
            gates = [groups[0][1]]
        elif at == 2 and ring > 2:
            own_steps, extra = own_steps + later, [groups[1][0]]
        back_types = [jnp.bfloat16 if step in (half, half + 1) else jnp.float32 for step in own_steps]
        with jax.named_scope(f"group_{at}"):
            act, own_cols, *back = group_call(
                after(spots, *gates),
                [sets[chip][step][0] for chip, step in entries],
                [sets[chip][step][1] for chip, step in entries],
                limits[: 1 + max(chip for chip, _ in entries)],
                entries,
                weight_in,
                weight_out,
                tile,
                share,
                back_types,
                extra,
                WEIGHTS.get(at, 1.0),
            )
        own_grads.update(zip(own_steps, back))
        if at == last and ring > 2:
            hops.append(chain(range(half + 1, ring), from_next, "sum_down"))
        if at == 1 and ring > 3:
            second_over_chips(own_cols, groups[0][2])
        wait = [one[0][1] for one in sets[1:]] if at == 0 else hops
        groups.append((act, own_cols, send(after(act, *wait), "dp", swap_cores, f"swap_{at}")))

    if ring > 1:
        hops.append(chain(range(half, 0, -1), from_last, "sum_up"))
    grad_weight_in, grad_weight_out = weights_call(groups, totals, 1.0 / blocks)
    own_grad = after(own_grads[0], grad_weight_in).astype(jnp.float32)
    for hop in hops:
        own_grad = own_grad + hop.astype(jnp.float32)
    branch_grad = norm_backward(own_grad, standard, row_scale, norm_gain)
    grad_input = (grad_out.astype(jnp.float32) + branch_grad).astype(jnp.bfloat16)

    return (grad_input, grad_weight_in, grad_weight_out)


def solution(mesh):
    in_specs = (
        P(("groups", "dp", "tensor"), None),
        P(("groups", "dp", "tensor"), None),
        P(),
        P(("groups", "dp")),
        P(("groups", "dp"), None),
        P(None, "tensor"),
        P("tensor", None),
    )
    out_specs = (
        P(("groups", "dp", "tensor"), None),
        P(("groups", "dp"), "tensor"),
        P(("groups", "tensor"), "dp"),
    )
    return jax.shard_map(shards, mesh=mesh, in_specs=in_specs, out_specs=out_specs, check_vma=False)
```

```python
import functools
import math

import jax
import jax.numpy as jnp
from jax import lax
from jax.experimental import pallas as pl
from jax.experimental.pallas import tpu as pltpu
from jax.sharding import PartitionSpec as P

GELU_SCALE = 0.7978845608028654
GELU_CUBE = 0.044715
NORM_EPS = 1e-06
VMEM_LIMIT = 48 * 1024 * 1024
WORK = 3.0
WEIGHTS = {1: 3.0, 3: 3.0}


def gelu_parts(pre_act):
    square = pre_act * pre_act
    tanh_val = jnp.tanh(pre_act * (GELU_SCALE + (GELU_SCALE * GELU_CUBE) * square))
    share = 0.5 + 0.5 * tanh_val
    gelu_value = pre_act * share
    gelu_slope = share + gelu_value * (1.0 - tanh_val) * (
        GELU_SCALE + (3.0 * GELU_SCALE * GELU_CUBE) * square
    )
    return (gelu_value, gelu_slope)


def unit_limits(block_order, count_row, first, unit_total):
    above_three = count_row[3]
    above_two = above_three + count_row[2]
    above_one = above_two + count_row[1]
    count = block_order.shape[0]
    places = jnp.arange(count, dtype=jnp.int32)
    ranked = (
        (places < above_three).astype(jnp.int32)
        + (places < above_two).astype(jnp.int32)
        + (places < above_one).astype(jnp.int32)
    )
    tokens = (first + places) % count
    hits = block_order[None, :] == tokens[:, None]
    limits = unit_total // (1 << (3 - ranked))
    return jnp.sum(jnp.where(hits, limits[None, :], 0), axis=1, keepdims=True)


def norm_backward(grad_normed, standard, row_scale, norm_gain):
    scaled = grad_normed * norm_gain[None, :]
    centre = jnp.mean(scaled, axis=1, keepdims=True)
    along = jnp.mean(scaled * standard, axis=1, keepdims=True)
    return row_scale * (scaled - centre - standard * along)


def work_of(flops):
    return pl.CostEstimate(flops=int(WORK * flops), bytes_accessed=0, transcendentals=0)


def tile_of(extent, wanted):
    while extent % wanted:
        wanted //= 2
    return wanted


def group_kernel(spots, *refs, limit_at, owned, extra, share, tiles):
    pieces, sets = len(limit_at), 1 + max(at for at, _ in limit_at)
    normed_refs = refs[:pieces]
    grad_refs = refs[pieces : 2 * pieces]
    limit_refs = refs[2 * pieces : 2 * pieces + sets]
    extra_refs = refs[2 * pieces + sets : 2 * pieces + sets + extra]
    in_ref, out_ref, acts_ref, own_ref, *rest = refs[2 * pieces + sets + extra :]
    tile = pl.program_id(0)

    def columns(target, first):
        span = pl.ds(pl.multiple_of(first, 128), share)
        for kind, sources in enumerate((normed_refs, grad_refs)):
            for at, ref in enumerate(sources):
                size = ref.shape[0]
                target[kind, at * size : (at + 1) * size, :] = ref[:, span]

    rows_ref, rest = rest[-1], rest[:-1]
    size = normed_refs[0].shape[0]
    limit = jnp.concatenate([limit_refs[at][step * size : (step + 1) * size, :] for at, step in limit_at])

    @pl.when(tile == 0)
    def _():
        columns(own_ref, spots[1])
        for kind, sources in enumerate((normed_refs, grad_refs)):
            for at, ref in enumerate(sources):
                size = ref.shape[0]
                rows_ref[kind, at * size : (at + 1) * size, :] = ref[...]

    @pl.when(tile == tiles)
    def _():
        columns(acts_ref, spots[2])

    @pl.when(tile < tiles)
    def _():
        group_tile(spots[0], rows_ref, limit, in_ref, out_ref, acts_ref, rest, owned * size, extra_refs, tiles)


def group_tile(
    first, rows_ref, limit, in_ref, out_ref, acts_ref, rest, own_rows, extra_refs, tiles
):
    tile = pl.program_id(0)
    units = in_ref.shape[1]
    width = 256 if units % 256 == 0 else units

    mask = first + tile * units < limit
    products = []
    for start in range(0, units, width):
        span = slice(start, start + width)
        pre_act = jnp.dot(rows_ref[0], in_ref[:, span], preferred_element_type=jnp.float32)
        grad_hidden = lax.dot_general(
            rows_ref[1], out_ref[span, :], (((1,), (1,)), ((), ())), preferred_element_type=jnp.float32
        )
        products.append((span, pre_act, grad_hidden))
    for span, pre_act, grad_hidden in products:
        gelu_value, gelu_slope = gelu_parts(pre_act)
        acts_ref[0, :, span] = jnp.where(mask, grad_hidden * gelu_slope, 0.0).astype(jnp.bfloat16)
        acts_ref[1, :, span] = jnp.where(mask, gelu_value, 0.0).astype(jnp.bfloat16)
    if rest:
        back_refs, total_ref = rest[:-1], rest[-1]
        parts = [acts_ref[0, :own_rows, :]] if own_rows else []
        term = lax.dot_general(
            jnp.concatenate(parts + [ref[0] for ref in extra_refs]),
            in_ref[...],
            (((1,), (1,)), ((), ())),
            preferred_element_type=jnp.float32,
        )

        @pl.when(tile == 0)
        def _():
            total_ref[...] = term

        @pl.when(tile != 0)
        def _():
            total_ref[...] += term

        @pl.when(tile == tiles - 1)
        def _():
            for at, ref in enumerate(back_refs):
                size = ref.shape[0]
                ref[...] = total_ref[at * size : (at + 1) * size, :].astype(ref.dtype)


def group_call(
    spots, normed, grads, limits, limit_at, weight_in, weight_out, tile, share, back_types, extra, weight
):
    features, units = weight_in.shape
    piece_rows = normed[0].shape[0]
    rows = piece_rows * len(normed)
    owned = len(back_types) - len(extra)
    tiles = units // tile
    whole = lambda shape: pl.BlockSpec(shape, lambda i, spots: (0,) * len(shape))
    out_shape = [
        jax.ShapeDtypeStruct((2, rows, units + share), jnp.bfloat16),
        jax.ShapeDtypeStruct((2, rows, share), jnp.bfloat16),
    ]
    out_specs = [
        pl.BlockSpec((2, rows, tile), lambda i, spots: (0, 0, i)),
        whole((2, rows, share)),
    ]
    for kind in back_types:
        out_shape.append(jax.ShapeDtypeStruct((piece_rows, features), kind))
        out_specs.append(whole((piece_rows, features)))
    return pl.pallas_call(
        functools.partial(
            group_kernel,
            limit_at=limit_at,
            owned=owned,
            extra=len(extra),
            share=share,
            tiles=tiles,
        ),
        grid_spec=pltpu.PrefetchScalarGridSpec(
            num_scalar_prefetch=1,
            grid=(tiles + share // tile,),
            in_specs=[whole(one.shape) for one in (*normed, *grads, *limits)]
            + [
                pl.BlockSpec((1, piece_rows, tile), lambda i, spots, at=at: (0, at, jnp.minimum(i, tiles - 1)))
                for _, at in extra
            ]
            + [
                pl.BlockSpec((features, tile), lambda i, spots: (0, jnp.minimum(i, tiles - 1))),
                pl.BlockSpec((tile, features), lambda i, spots: (jnp.minimum(i, tiles - 1), 0)),
            ],
            out_specs=out_specs,
            scratch_shapes=[pltpu.VMEM((len(back_types) * piece_rows, features), jnp.float32)]
            * bool(back_types)
            + [pltpu.VMEM((2, rows, features), jnp.bfloat16)],
        ),
        out_shape=out_shape,
        compiler_params=pltpu.CompilerParams(vmem_limit_bytes=VMEM_LIMIT),
        cost_estimate=work_of(weight * (4 * rows + 2 * len(back_types) * piece_rows) * units * features),
        name="group",
    )(spots, *normed, *grads, *limits, *(one for one, _ in extra), weight_in, weight_out)


def weights_kernel(*refs, groups, scale, started):
    act_refs = refs[:groups]
    col_refs = refs[groups : 2 * groups]
    in_ref, out_ref = refs[-2:]

    def stack(sources, kind):
        return jnp.concatenate([ref[kind] for ref in sources], axis=0)

    def total(left, right):
        return lax.dot_general(
            left, right, (((0,), (0,)), ((), ())), preferred_element_type=jnp.float32
        )

    for_in = total(stack(col_refs, 0), stack(act_refs, 0))
    for_out = total(stack(act_refs, 1), stack(col_refs, 1))
    if started:
        for_in += refs[-4][...].astype(jnp.float32)
        for_out += refs[-3][...].astype(jnp.float32)
    in_ref[...] = (for_in * scale).astype(in_ref.dtype)
    out_ref[...] = (for_out * scale).astype(out_ref.dtype)


def weights_call(groups, begun, scale):
    share = groups[0][1].shape[2]
    units = groups[0][0].shape[2] - share
    tile = tile_of(units, 512)
    acts, acts_specs, cols, cols_specs = [], [], [], []
    for own, own_cols, other in groups:
        rows = own.shape[1]
        acts += [own, other]
        acts_specs += [pl.BlockSpec((2, rows, tile), lambda i: (0, 0, i))] * 2
        cols += [own_cols, other]
        cols_specs += [
            pl.BlockSpec((2, rows, share), lambda i: (0, 0, 0)),
            pl.BlockSpec((2, rows, share), lambda i: (0, 0, units // share)),
        ]
    in_spec = pl.BlockSpec((share, tile), lambda i: (0, i))
    out_spec = pl.BlockSpec((tile, share), lambda i: (i, 0))
    return pl.pallas_call(
        functools.partial(weights_kernel, groups=len(acts), scale=scale, started=bool(begun)),
        grid=(units // tile,),
        in_specs=acts_specs + cols_specs + ([in_spec, out_spec] if begun else []),
        out_specs=[in_spec, out_spec],
        out_shape=[
            jax.ShapeDtypeStruct((share, units), jnp.bfloat16),
            jax.ShapeDtypeStruct((units, share), jnp.bfloat16),
        ],
        compiler_params=pltpu.CompilerParams(vmem_limit_bytes=VMEM_LIMIT),
        cost_estimate=work_of(0),
        name="weights",
    )(*acts, *cols, *begun)


def after(value, *others):
    return lax.optimization_barrier((value, others))[0] if others else value


def shards(inputs, grad_out, norm_gain, level_order, level_counts, weight_in, weight_out):
    rows = inputs.shape[0]
    ring = lax.axis_size("tensor")
    place = lax.axis_index("tensor")
    blocks = lax.axis_size("dp")
    block = lax.axis_index("dp")
    chips = blocks // 2
    unit_local = weight_in.shape[1]
    unit_total = unit_local * ring
    share = inputs.shape[1] // blocks
    tile = math.gcd(unit_local, unit_total // 8, share)

    from_next = [((i + 1) % ring, i) for i in range(ring)]
    from_last = [(i, (i + 1) % ring) for i in range(ring)]
    from_chip = [((i + 2) % blocks, i) for i in range(blocks)]
    swap_cores = [(i, i ^ 1) for i in range(blocks)]
    half = ring // 2

    def send(one, axis, pairs, name):
        with jax.named_scope(name):
            return lax.ppermute(one, axis, pairs)

    as_float = inputs.astype(jnp.float32)
    row_mean = jnp.mean(as_float, axis=1, keepdims=True)
    centred = as_float - row_mean
    row_scale = lax.rsqrt(jnp.mean(centred * centred, axis=1, keepdims=True) + NORM_EPS)
    standard = centred * row_scale
    normed = (standard * norm_gain[None, :]).astype(jnp.bfloat16)

    limits = [unit_limits(level_order, level_counts[0], place * rows, unit_total)]
    for _ in range(1, chips):
        limits.append(send(limits[-1], "dp", from_chip, "chip_limits"))

    spots = jnp.stack([place * unit_local, block * share, (block ^ 1) * share]).astype(jnp.int32)

    kinds = ("normed", "grad")

    def move(piece, axis, pairs, name, *gates):
        return tuple(
            send(after(one, *gates), axis, pairs, f"{name}_{kind}") for one, kind in zip(piece, kinds)
        )

    near = {0: (normed, grad_out)}
    for step in range(1, ring):
        near[step] = move(near[step - 1], "tensor", from_next, f"ring_{step}")
    sets = [[near[step] for step in range(ring)]]
    for chip in range(1, chips):
        far = []
        for step, piece in enumerate(sets[-1]):
            if step == 0:
                piece = (piece[0], after(piece[1], *limits[1:]))
            far.append(None if step == ring - 1 else move(piece, "dp", from_chip, f"chip_{step}"))
        sets.append(far)

    def last_over_chips(early, gates):
        for chip in range(1, chips):
            normed_rows, grads = sets[chip - 1][-1]
            name = f"chip_{ring - 1}"
            grads = send(after(grads, *gates), "dp", from_chip, f"{name}_grad")
            normed_rows = send(after(normed_rows, *early), "dp", from_chip, f"{name}_normed")
            sets[chip][-1] = (normed_rows, grads)

    groups, own_grads, hops, hold = [], {}, [], []

    def chain(steps, pairs, name):
        travelling = None
        for step in steps:
            total = after(own_grads[step], *hold)
            if travelling is not None:
                total = (total + travelling.astype(jnp.float32)).astype(jnp.bfloat16)
            travelling = send(total.astype(jnp.bfloat16), "tensor", pairs, f"{name}_{step}")
        return travelling

    arrivals = [
        [(chip, slot - chip) for chip in range(chips) if 0 <= slot - chip < ring]
        for slot in range(ring + chips - 1)
    ]
    if len(arrivals) > 1:
        arrivals[:2] = [sorted(arrivals[0] + arrivals[1])]
    last = len(arrivals) - 1
    totals = []
    for at, entries in enumerate(arrivals):
        gates = []
        if at == len(arrivals) - 2 and at > 1:
            totals = weights_call(groups[:-1], [], 1.0)
            gates = hold = [totals[0]]
            groups = groups[-1:]
        if not hold and at > 1:
            hold = [own_cols]
        if any(sets[chip][step] is None for chip, step in arrivals[min(at + 1, last)]):
            last_over_chips([own_cols], hold)
        own_steps = [step for chip, step in entries if chip == 0]
        extra = []
        if at == 0 and ring > 2:
            own_steps = own_steps[:1]
        elif at == 1 and ring > 2:
            own_steps, extra = own_steps + [1], [(groups[0][0], 1)]
        back_types = [jnp.bfloat16 if step in (half, half + 1) else jnp.float32 for step in own_steps]
        with jax.named_scope(f"group_{at}"):
            act, own_cols, *back = group_call(
                after(spots, *gates),
                [sets[chip][step][0] for chip, step in entries],
                [sets[chip][step][1] for chip, step in entries],
                limits[: 1 + max(chip for chip, _ in entries)],
                entries,
                weight_in,
                weight_out,
                tile,
                share,
                back_types,
                extra,
                WEIGHTS.get(at, 1.0),
            )
        own_grads.update(zip(own_steps, back))
        if at == last and ring > 2:
            hops.append(chain(range(half + 1, ring), from_next, "sum_down"))
        groups.append((act, own_cols, send(after(act, *hops), "dp", swap_cores, f"swap_{at}")))

    if ring > 1:
        hops.append(chain(range(half, 0, -1), from_last, "sum_up"))
    grad_weight_in, grad_weight_out = weights_call(groups, totals, 1.0 / blocks)
    own_grad = after(own_grads[0], grad_weight_in).astype(jnp.float32)
    for hop in hops:
        own_grad = own_grad + hop.astype(jnp.float32)
    branch_grad = norm_backward(own_grad, standard, row_scale, norm_gain)
    grad_input = (grad_out.astype(jnp.float32) + branch_grad).astype(jnp.bfloat16)

    return (grad_input, grad_weight_in, grad_weight_out)


def solution(mesh):
    in_specs = (
        P(("groups", "dp", "tensor"), None),
        P(("groups", "dp", "tensor"), None),
        P(),
        P(("groups", "dp")),
        P(("groups", "dp"), None),
        P(None, "tensor"),
        P("tensor", None),
    )
    out_specs = (
        P(("groups", "dp", "tensor"), None),
        P(("groups", "dp"), "tensor"),
        P(("groups", "tensor"), "dp"),
    )
    return jax.shard_map(shards, mesh=mesh, in_specs=in_specs, out_specs=out_specs, check_vma=False)
```

```python
import functools
import math

import jax
import jax.numpy as jnp
from jax import lax
from jax.experimental import pallas as pl
from jax.experimental.pallas import tpu as pltpu
from jax.sharding import PartitionSpec as P

GELU_SCALE = 0.7978845608028654
GELU_CUBE = 0.044715
NORM_EPS = 1e-06
VMEM_LIMIT = 48 * 1024 * 1024
WORK = 3.0
WEIGHTS = {1: 3.0, 3: 3.0}


def gelu_parts(pre_act):
    square = pre_act * pre_act
    tanh_val = jnp.tanh(pre_act * (GELU_SCALE + (GELU_SCALE * GELU_CUBE) * square))
    share = 0.5 + 0.5 * tanh_val
    gelu_value = pre_act * share
    gelu_slope = share + gelu_value * (1.0 - tanh_val) * (
        GELU_SCALE + (3.0 * GELU_SCALE * GELU_CUBE) * square
    )
    return (gelu_value, gelu_slope)


def unit_limits(block_order, count_row, first, unit_total):
    above_three = count_row[3]
    above_two = above_three + count_row[2]
    above_one = above_two + count_row[1]
    count = block_order.shape[0]
    places = jnp.arange(count, dtype=jnp.int32)
    ranked = (
        (places < above_three).astype(jnp.int32)
        + (places < above_two).astype(jnp.int32)
        + (places < above_one).astype(jnp.int32)
    )
    tokens = (first + places) % count
    hits = block_order[None, :] == tokens[:, None]
    limits = unit_total // (1 << (3 - ranked))
    return jnp.sum(jnp.where(hits, limits[None, :], 0), axis=1, keepdims=True)


def norm_backward(grad_normed, standard, row_scale, norm_gain):
    scaled = grad_normed * norm_gain[None, :]
    centre = jnp.mean(scaled, axis=1, keepdims=True)
    along = jnp.mean(scaled * standard, axis=1, keepdims=True)
    return row_scale * (scaled - centre - standard * along)


def work_of(flops):
    return pl.CostEstimate(flops=int(WORK * flops), bytes_accessed=0, transcendentals=0)


def tile_of(extent, wanted):
    while extent % wanted:
        wanted //= 2
    return wanted


def group_kernel(spots, *refs, limit_at, owned, share, tiles):
    pieces, sets = len(limit_at), 1 + max(at for at, _ in limit_at)
    normed_refs = refs[:pieces]
    grad_refs = refs[pieces : 2 * pieces]
    limit_refs = refs[2 * pieces : 2 * pieces + sets]
    in_ref, out_ref, acts_ref, own_ref, *rest = refs[2 * pieces + sets :]
    tile = pl.program_id(0)

    def columns(target, first):
        span = pl.ds(pl.multiple_of(first, 128), share)
        for kind, sources in enumerate((normed_refs, grad_refs)):
            for at, ref in enumerate(sources):
                size = ref.shape[0]
                target[kind, at * size : (at + 1) * size, :] = ref[:, span]

    rows_ref, rest = rest[-1], rest[:-1]
    size = normed_refs[0].shape[0]
    limit = jnp.concatenate([limit_refs[at][step * size : (step + 1) * size, :] for at, step in limit_at])

    @pl.when(tile == 0)
    def _():
        columns(own_ref, spots[1])
        for kind, sources in enumerate((normed_refs, grad_refs)):
            for at, ref in enumerate(sources):
                size = ref.shape[0]
                rows_ref[kind, at * size : (at + 1) * size, :] = ref[...]

    @pl.when(tile == tiles)
    def _():
        columns(acts_ref, spots[2])

    @pl.when(tile < tiles)
    def _():
        group_tile(spots[0], rows_ref, limit, in_ref, out_ref, acts_ref, rest, owned, tiles)


def group_tile(first, rows_ref, limit, in_ref, out_ref, acts_ref, rest, owned, tiles):
    tile = pl.program_id(0)
    units = in_ref.shape[1]
    width = 256 if units % 256 == 0 else units

    mask = first + tile * units < limit
    products = []
    for start in range(0, units, width):
        span = slice(start, start + width)
        pre_act = jnp.dot(rows_ref[0], in_ref[:, span], preferred_element_type=jnp.float32)
        grad_hidden = lax.dot_general(
            rows_ref[1], out_ref[span, :], (((1,), (1,)), ((), ())), preferred_element_type=jnp.float32
        )
        products.append((span, pre_act, grad_hidden))
    for span, pre_act, grad_hidden in products:
        gelu_value, gelu_slope = gelu_parts(pre_act)
        acts_ref[0, :, span] = jnp.where(mask, grad_hidden * gelu_slope, 0.0).astype(jnp.bfloat16)
        acts_ref[1, :, span] = jnp.where(mask, gelu_value, 0.0).astype(jnp.bfloat16)
    if owned:
        back_refs, total_ref = rest[:-1], rest[-1]
        term = lax.dot_general(
            acts_ref[0, : total_ref.shape[0], :],
            in_ref[...],
            (((1,), (1,)), ((), ())),
            preferred_element_type=jnp.float32,
        )

        @pl.when(tile == 0)
        def _():
            total_ref[...] = term

        @pl.when(tile != 0)
        def _():
            total_ref[...] += term

        @pl.when(tile == tiles - 1)
        def _():
            for at, ref in enumerate(back_refs):
                size = ref.shape[0]
                ref[...] = total_ref[at * size : (at + 1) * size, :].astype(ref.dtype)


def group_call(
    spots, normed, grads, limits, limit_at, weight_in, weight_out, tile, share, back_types, weight
):
    features, units = weight_in.shape
    piece_rows = normed[0].shape[0]
    rows = piece_rows * len(normed)
    owned = len(back_types)
    tiles = units // tile
    whole = lambda shape: pl.BlockSpec(shape, lambda i, spots: (0,) * len(shape))
    out_shape = [
        jax.ShapeDtypeStruct((2, rows, units + share), jnp.bfloat16),
        jax.ShapeDtypeStruct((2, rows, share), jnp.bfloat16),
    ]
    out_specs = [
        pl.BlockSpec((2, rows, tile), lambda i, spots: (0, 0, i)),
        whole((2, rows, share)),
    ]
    for kind in back_types:
        out_shape.append(jax.ShapeDtypeStruct((piece_rows, features), kind))
        out_specs.append(whole((piece_rows, features)))
    return pl.pallas_call(
        functools.partial(
            group_kernel, limit_at=limit_at, owned=owned, share=share, tiles=tiles
        ),
        grid_spec=pltpu.PrefetchScalarGridSpec(
            num_scalar_prefetch=1,
            grid=(tiles + share // tile,),
            in_specs=[whole(one.shape) for one in (*normed, *grads, *limits)]
            + [
                pl.BlockSpec((features, tile), lambda i, spots: (0, jnp.minimum(i, tiles - 1))),
                pl.BlockSpec((tile, features), lambda i, spots: (jnp.minimum(i, tiles - 1), 0)),
            ],
            out_specs=out_specs,
            scratch_shapes=[pltpu.VMEM((owned * piece_rows, features), jnp.float32)] * bool(owned)
            + [pltpu.VMEM((2, rows, features), jnp.bfloat16)],
        ),
        out_shape=out_shape,
        compiler_params=pltpu.CompilerParams(vmem_limit_bytes=VMEM_LIMIT),
        cost_estimate=work_of(weight * (4 * rows + 2 * owned * piece_rows) * units * features),
        name="group",
    )(spots, *normed, *grads, *limits, weight_in, weight_out)


def weights_kernel(*refs, groups, scale, started):
    act_refs = refs[:groups]
    col_refs = refs[groups : 2 * groups]
    in_ref, out_ref = refs[-2:]

    def stack(sources, kind):
        return jnp.concatenate([ref[kind] for ref in sources], axis=0)

    def total(left, right):
        return lax.dot_general(
            left, right, (((0,), (0,)), ((), ())), preferred_element_type=jnp.float32
        )

    for_in = total(stack(col_refs, 0), stack(act_refs, 0))
    for_out = total(stack(act_refs, 1), stack(col_refs, 1))
    if started:
        for_in += refs[-4][...].astype(jnp.float32)
        for_out += refs[-3][...].astype(jnp.float32)
    in_ref[...] = (for_in * scale).astype(in_ref.dtype)
    out_ref[...] = (for_out * scale).astype(out_ref.dtype)


def weights_call(groups, begun, scale):
    share = groups[0][1].shape[2]
    units = groups[0][0].shape[2] - share
    tile = tile_of(units, 512)
    acts, acts_specs, cols, cols_specs = [], [], [], []
    for own, own_cols, other in groups:
        rows = own.shape[1]
        acts += [own, other]
        acts_specs += [pl.BlockSpec((2, rows, tile), lambda i: (0, 0, i))] * 2
        cols += [own_cols, other]
        cols_specs += [
            pl.BlockSpec((2, rows, share), lambda i: (0, 0, 0)),
            pl.BlockSpec((2, rows, share), lambda i: (0, 0, units // share)),
        ]
    in_spec = pl.BlockSpec((share, tile), lambda i: (0, i))
    out_spec = pl.BlockSpec((tile, share), lambda i: (i, 0))
    return pl.pallas_call(
        functools.partial(weights_kernel, groups=len(acts), scale=scale, started=bool(begun)),
        grid=(units // tile,),
        in_specs=acts_specs + cols_specs + ([in_spec, out_spec] if begun else []),
        out_specs=[in_spec, out_spec],
        out_shape=[
            jax.ShapeDtypeStruct((share, units), jnp.bfloat16),
            jax.ShapeDtypeStruct((units, share), jnp.bfloat16),
        ],
        compiler_params=pltpu.CompilerParams(vmem_limit_bytes=VMEM_LIMIT),
        cost_estimate=work_of(0),
        name="weights",
    )(*acts, *cols, *begun)


def after(value, *others):
    return lax.optimization_barrier((value, others))[0] if others else value


def shards(inputs, grad_out, norm_gain, level_order, level_counts, weight_in, weight_out):
    rows = inputs.shape[0]
    ring = lax.axis_size("tensor")
    place = lax.axis_index("tensor")
    blocks = lax.axis_size("dp")
    block = lax.axis_index("dp")
    chips = blocks // 2
    unit_local = weight_in.shape[1]
    unit_total = unit_local * ring
    share = inputs.shape[1] // blocks
    tile = math.gcd(unit_local, unit_total // 8, share)

    from_next = [((i + 1) % ring, i) for i in range(ring)]
    from_last = [(i, (i + 1) % ring) for i in range(ring)]
    from_chip = [((i + 2) % blocks, i) for i in range(blocks)]
    swap_cores = [(i, i ^ 1) for i in range(blocks)]
    half = ring // 2

    def send(one, axis, pairs, name):
        with jax.named_scope(name):
            return lax.ppermute(one, axis, pairs)

    level_sets = [jnp.concatenate([level_order, level_counts[0]])]
    for _ in range(1, chips):
        level_sets.append(send(level_sets[-1], "dp", from_chip, "chip_levels"))

    as_float = inputs.astype(jnp.float32)
    row_mean = jnp.mean(as_float, axis=1, keepdims=True)
    centred = as_float - row_mean
    row_scale = lax.rsqrt(jnp.mean(centred * centred, axis=1, keepdims=True) + NORM_EPS)
    standard = centred * row_scale
    normed = (standard * norm_gain[None, :]).astype(jnp.bfloat16)

    limits = [unit_limits(one[:-4], one[-4:], place * rows, unit_total) for one in level_sets]
    spots = jnp.stack([place * unit_local, block * share, (block ^ 1) * share]).astype(jnp.int32)

    kinds = ("normed", "grad")

    def move(piece, axis, pairs, name, *gates):
        return tuple(
            send(after(one, *gates), axis, pairs, f"{name}_{kind}") for one, kind in zip(piece, kinds)
        )

    near = {0: (normed, grad_out)}
    for step in range(1, ring):
        near[step] = move(near[step - 1], "tensor", from_next, f"ring_{step}")
    sets = [[near[step] for step in range(ring)]]
    for chip in range(1, chips):
        far = []
        for step, piece in enumerate(sets[-1]):
            if step == 0:
                piece = (after(piece[0], *level_sets[1:]), piece[1])
            far.append(None if step == ring - 1 else move(piece, "dp", from_chip, f"chip_{step}"))
        sets.append(far)

    def last_over_chips(early, gates):
        for chip in range(1, chips):
            normed_rows, grads = sets[chip - 1][-1]
            name = f"chip_{ring - 1}"
            grads = send(after(grads, *gates), "dp", from_chip, f"{name}_grad")
            normed_rows = send(after(normed_rows, *early), "dp", from_chip, f"{name}_normed")
            sets[chip][-1] = (normed_rows, grads)

    groups, own_grads, hops, hold = [], [], [], []

    def chain(steps, pairs, name):
        travelling = None
        for step in steps:
            total = after(own_grads[step], *hold)
            if travelling is not None:
                total = (total + travelling.astype(jnp.float32)).astype(jnp.bfloat16)
            travelling = send(total.astype(jnp.bfloat16), "tensor", pairs, f"{name}_{step}")
        return travelling

    arrivals = [
        [(chip, slot - chip) for chip in range(chips) if 0 <= slot - chip < ring]
        for slot in range(ring + chips - 1)
    ]
    if len(arrivals) > 1:
        arrivals[:2] = [sorted(arrivals[0] + arrivals[1])]
    last = len(arrivals) - 1
    totals = []
    for at, entries in enumerate(arrivals):
        gates = []
        if at == len(arrivals) - 2 and at > 1:
            totals = weights_call(groups[:-1], [], 1.0)
            gates = hold = [totals[0]]
            groups = groups[-1:]
        if not hold and at > 1:
            hold = [own_cols]
        if any(sets[chip][step] is None for chip, step in arrivals[min(at + 1, last)]):
            last_over_chips([own_cols], hold)
        own_steps = [step for chip, step in entries if chip == 0]
        back_types = [jnp.bfloat16 if step in (half, half + 1) else jnp.float32 for step in own_steps]
        with jax.named_scope(f"group_{at}"):
            act, own_cols, *back = group_call(
                after(spots, *gates),
                [sets[chip][step][0] for chip, step in entries],
                [sets[chip][step][1] for chip, step in entries],
                limits[: 1 + max(chip for chip, _ in entries)],
                entries,
                weight_in,
                weight_out,
                tile,
                share,
                back_types,
                WEIGHTS.get(at, 1.0),
            )
        own_grads.extend(back)
        if at == last and ring > 2:
            hops.append(chain(range(half + 1, ring), from_next, "sum_down"))
        groups.append((act, own_cols, send(after(act, *hops), "dp", swap_cores, f"swap_{at}")))

    if ring > 1:
        hops.append(chain(range(half, 0, -1), from_last, "sum_up"))
    grad_weight_in, grad_weight_out = weights_call(groups, totals, 1.0 / blocks)
    own_grad = after(own_grads[0], grad_weight_in).astype(jnp.float32)
    for hop in hops:
        own_grad = own_grad + hop.astype(jnp.float32)
    branch_grad = norm_backward(own_grad, standard, row_scale, norm_gain)
    grad_input = (grad_out.astype(jnp.float32) + branch_grad).astype(jnp.bfloat16)

    return (grad_input, grad_weight_in, grad_weight_out)


def solution(mesh):
    in_specs = (
        P(("groups", "dp", "tensor"), None),
        P(("groups", "dp", "tensor"), None),
        P(),
        P(("groups", "dp")),
        P(("groups", "dp"), None),
        P(None, "tensor"),
        P("tensor", None),
    )
    out_specs = (
        P(("groups", "dp", "tensor"), None),
        P(("groups", "dp"), "tensor"),
        P(("groups", "tensor"), "dp"),
    )
    return jax.shard_map(shards, mesh=mesh, in_specs=in_specs, out_specs=out_specs, check_vma=False)
```
